32 devices in a mesh: gx: 4 (over z), gy: 4 (over y, x), gz: 2 (over core).
Axes of the slice: x: 2, y: 2, z: 4, core: 2. Of those that a mesh axis runs over, the one named last changes fastest.
Arguments:
- fine_state: float32 [64, 5, 32, 1024], P(('gx', 'gy', 'gz')), may hold values from -1.2 to 3.5, as said below
- coarse_state: float32 [128, 5, 16, 256], P(('gx', 'gy', 'gz')), may hold values from -1.2 to 3.5, as said below
- neighbours: int32 [64, 6], P(('gx', 'gy', 'gz')), may hold values from -1 to 63, as said below
- coarse_sources: int32 [64, 6], P(('gx', 'gy', 'gz')), may hold values from -1 to 127, as said below
- covering: int32 [128], P(('gx', 'gy', 'gz')), may hold values from -1 to 63, as said below
Outputs:
- fine_next: float32 [64, 5, 32, 1024], P(('gx', 'gy', 'gz'))
- coarse_next: float32 [128, 5, 16, 256], P(('gx', 'gy', 'gz'))
The draws below stay inside these ranges and needn't reach their ends.
Inputs may be any that keep to these rules, and one draw needn't show every extreme that they name: `fine_state`: each cell is the conserved state of density 0.5 to 2, velocity components -0.6 to 0.6 and pressure 0.4 to 1.6. `coarse_state`: each cell is the conserved state of density 0.5 to 2, velocity components -0.6 to 0.6 and pressure 0.4 to 1.6. For each box face exactly one of neighbours and coarse_sources is not -1; every box or block named lies on a device with the same gx index as the box; the faces of one device's boxes name at most 2 boxes or blocks held by any one device, and exactly 2 on some device. `coarse_sources`: see neighbours. `covering`: every fine box is named by exactly one block; a block and the box it names lie on devices with the same gy and gz index; the blocks of one device name at most 1 boxes of any one device, and exactly 1 of some device.
All inputs are finite; a program needn't handle non-finite values.
Results may differ from the reference program's by a relative error of at most 0.00005.
Values sent between devices are 32-bit elements; how exact they have to be, the bound alone decides.
A program may use at most 64 MiB of HBM per device.

```python
import math
import jax
import jax.numpy as jnp
from jax import lax

EDGE = 32
HALF = 16
BOX_DEV = 2
CB_DEV = 4
BOXES = 64
CBLOCKS = 128
N_GX = 4
N_GY = 4
N_GZ = 2
DEVICES = 32


adiabatic = 5.0 / 3.0


def conserved(key, item_count, row_count, width):
    subkeys = jax.random.split(key, 3)
    cell_shape = (item_count, row_count, width)
    density = jnp.exp(jax.random.uniform(subkeys[0], cell_shape, jnp.float32, math.log(0.5), math.log(2.0)))
    velocity = 0.25 * jax.random.truncated_normal(subkeys[1], -2.4, 2.4, (3,) + cell_shape, jnp.float32)
    pressure = jnp.exp(jax.random.uniform(subkeys[2], cell_shape, jnp.float32, math.log(0.4), math.log(1.6)))
    momentum = density[None] * velocity
    energy = pressure / (adiabatic - 1.0) + 0.5 * density * jnp.sum(velocity * velocity, axis=0)
    return jnp.stack([density, momentum[0], momentum[1], momentum[2], energy], axis=1)


def draw_fine_state(key, part):
    return conserved(jax.random.fold_in(key, 3), BOXES, EDGE, EDGE * EDGE)


def draw_coarse_state(key, part):
    return conserved(jax.random.fold_in(key, 5), CBLOCKS, HALF, HALF * HALF)


def face_sources(key):
    line_size = N_GY * N_GZ
    face_count = 6 * BOX_DEV
    per_peer = (face_count + line_size - 1) // line_size
    subkeys = jax.random.split(jax.random.fold_in(key, 11), 5)
    peer_keys = jax.random.split(subkeys[0], DEVICES)
    peer_order = jax.vmap(lambda subkey: jax.random.permutation(subkey, line_size))(peer_keys)
    face_keys = jax.random.split(subkeys[1], DEVICES)
    face_order = jax.vmap(lambda subkey: jax.random.permutation(subkey, face_count))(face_keys)
    sequence = jnp.broadcast_to(jnp.arange(face_count, dtype=jnp.int32) // per_peer, (DEVICES, face_count))
    peer_seq = jnp.take_along_axis(peer_order, sequence, axis=1)
    peer_face = jnp.take_along_axis(peer_seq, jnp.argsort(face_order, axis=1), axis=1)
    devices = jnp.arange(DEVICES, dtype=jnp.int32)
    source_dev = (devices // line_size)[:, None] * line_size + peer_face
    fine_face = jax.random.randint(subkeys[2], (DEVICES, face_count), 0, 2)
    fine_pick = jax.random.randint(subkeys[3], (DEVICES, face_count), 0, BOX_DEV)
    coarse_pick = jax.random.randint(subkeys[4], (DEVICES, face_count), 0, CB_DEV)
    fine_ids = jnp.where(fine_face == 1, source_dev * BOX_DEV + fine_pick, -1)
    coarse_ids = jnp.where(fine_face == 0, source_dev * CB_DEV + coarse_pick, -1)
    return (fine_ids.reshape(BOXES, 6).astype(jnp.int32), coarse_ids.reshape(BOXES, 6).astype(jnp.int32))


def draw_neighbours(key, part):
    return face_sources(key)[0]


def draw_coarse_sources(key, part):
    return face_sources(key)[1]


def draw_covering(key, part):
    line_size = N_GY * N_GZ
    per_pair = (BOX_DEV + N_GX - 1) // N_GX
    subkeys = jax.random.split(jax.random.fold_in(key, 23), 4)
    weight = 1 + jax.random.randint(subkeys[0], (line_size, 1, N_GX), 0, 4) ** 2
    scores = jax.random.randint(subkeys[1], (line_size, N_GX, N_GX), 0, 1024) * weight
    scores = scores * N_GX + jnp.arange(N_GX, dtype=jnp.int32)
    target_order = jnp.argsort(-scores, axis=2)
    pick_index = jnp.arange(BOX_DEV, dtype=jnp.int32) // per_pair
    target = target_order[:, :, pick_index]
    slot_keys = jax.random.split(subkeys[2], line_size * N_GX)
    slot_order = jax.vmap(lambda subkey: jax.random.permutation(subkey, BOX_DEV))(slot_keys).reshape(line_size, N_GX * BOX_DEV)
    flat_target = target.reshape(line_size, N_GX * BOX_DEV)
    hits = (flat_target[:, :, None] == jnp.arange(N_GX, dtype=jnp.int32)[None, None, :]).astype(jnp.int32)
    arrival = jnp.sum((jnp.cumsum(hits, axis=1) - hits) * hits, axis=2)
    block_keys = jax.random.split(subkeys[3], line_size * N_GX)
    block_order = jax.vmap(lambda subkey: jax.random.permutation(subkey, CB_DEV))(block_keys).reshape(line_size, N_GX, CB_DEV)
    lines = jnp.arange(line_size, dtype=jnp.int32)[:, None]
    block_slot = block_order[lines, flat_target, arrival]
    sender = jnp.broadcast_to(jnp.arange(N_GX, dtype=jnp.int32)[None, :, None], (line_size, N_GX, BOX_DEV)).reshape(line_size, N_GX * BOX_DEV)
    fine_ids = (sender * line_size + lines) * BOX_DEV + slot_order
    coarse_rows = (flat_target * line_size + lines) * CB_DEV + block_slot
    covering = jnp.full((CBLOCKS,), -1, jnp.int32)
    return covering.at[coarse_rows.reshape(-1)].set(fine_ids.reshape(-1).astype(jnp.int32))


def setup_inputs(seed: int = 0) -> dict:
    splits = jax.random.split(jax.random.key(seed), 6)
    return {
        "fine_state": draw_fine_state(jax.random.fold_in(splits[5], 71), 0),
        "coarse_state": draw_coarse_state(jax.random.fold_in(splits[5], 71), 0),
        "neighbours": draw_neighbours(jax.random.fold_in(splits[5], 71), 0),
        "coarse_sources": draw_coarse_sources(jax.random.fold_in(splits[5], 71), 0),
        "covering": draw_covering(jax.random.fold_in(splits[5], 71), 0),
    }


adiabatic = 5.0 / 3.0
courant = 0.12

def edge_flux(left_state, right_state, normal):
    fluxes = []
    speeds = []
    for current in (left_state, right_state):
        density = current[0]
        normal_speed = current[normal] / density
        kinetic = 0.5 * (current[1] * current[1] + current[2] * current[2] + current[3] * current[3]) / density
        pressure = (adiabatic - 1.0) * (current[4] - kinetic)
        sound_speed = jnp.sqrt(adiabatic * pressure / density)
        entries = [current[normal], current[1] * normal_speed, current[2] * normal_speed, current[3] * normal_speed, (current[4] + pressure) * normal_speed]
        entries[normal] = entries[normal] + pressure
        fluxes.append(jnp.stack(entries))
        speeds.append(jnp.abs(normal_speed) + sound_speed)
    fastest = jnp.maximum(speeds[0], speeds[1])
    return 0.5 * (fluxes[0] + fluxes[1]) - 0.5 * fastest * (right_state - left_state)

def face_layers(cubes):
    return [cubes[:, :, 0], cubes[:, :, -1], cubes[:, :, :, 0], cubes[:, :, :, -1], cubes[:, :, :, :, 0], cubes[:, :, :, :, -1]]

def advance(box_cells, ghosts):
    padded = jnp.pad(box_cells, ((0, 0), (1, 1), (1, 1), (1, 1)))
    padded = padded.at[:, 0, 1:-1, 1:-1].set(ghosts[0])
    padded = padded.at[:, -1, 1:-1, 1:-1].set(ghosts[1])
    padded = padded.at[:, 1:-1, 0, 1:-1].set(ghosts[2])
    padded = padded.at[:, 1:-1, -1, 1:-1].set(ghosts[3])
    padded = padded.at[:, 1:-1, 1:-1, 0].set(ghosts[4])
    padded = padded.at[:, 1:-1, 1:-1, -1].set(ghosts[5])
    flux_x = edge_flux(padded[:, :-1, 1:-1, 1:-1], padded[:, 1:, 1:-1, 1:-1], 1)
    step_x = flux_x[:, 1:] - flux_x[:, :-1]
    flux_y = edge_flux(padded[:, 1:-1, :-1, 1:-1], padded[:, 1:-1, 1:, 1:-1], 2)
    step_y = flux_y[:, :, 1:] - flux_y[:, :, :-1]
    flux_z = edge_flux(padded[:, 1:-1, 1:-1, :-1], padded[:, 1:-1, 1:-1, 1:], 3)
    step_z = flux_z[:, :, :, 1:] - flux_z[:, :, :, :-1]
    return box_cells - courant * (step_x + step_y + step_z)

def reference(fine_state, coarse_state, neighbours, coarse_sources, covering):
    fine_cubes = fine_state.reshape(BOXES, 5, EDGE, EDGE, EDGE)
    coarse_cubes = coarse_state.reshape(CBLOCKS, 5, HALF, HALF, HALF)
    fine_faces = face_layers(fine_cubes)
    coarse_faces = [jnp.repeat(jnp.repeat(layer, 2, axis=2), 2, axis=3) for layer in face_layers(coarse_cubes)]
    ghost_list = []
    for face_side in range(6):
        opposite = face_side ^ 1
        from_fine = jnp.take(fine_faces[opposite], jnp.maximum(neighbours[:, face_side], 0), axis=0)
        from_coarse = jnp.take(coarse_faces[opposite], jnp.maximum(coarse_sources[:, face_side], 0), axis=0)
        ghost_list.append(jnp.where(neighbours[:, face_side][:, None, None, None] >= 0, from_fine, from_coarse))
    updated = lax.map(lambda packed: advance(packed[0], packed[1:]), (fine_cubes,) + tuple(ghost_list))
    averaged = updated.reshape(BOXES, 5, HALF, 2, HALF, 2, HALF, 2).mean(axis=(3, 5, 7))
    picked = jnp.take(averaged, jnp.maximum(covering, 0), axis=0)
    coarse_next = jnp.where(covering[:, None, None, None, None] >= 0, picked, coarse_cubes)
    return (updated.reshape(BOXES, 5, EDGE, EDGE * EDGE), coarse_next.reshape(CBLOCKS, 5, HALF, HALF * HALF))
```

```python
import functools
import jax
import jax.numpy as jnp
from jax import lax
from jax.experimental import pallas as pl
from jax.experimental.pallas import tpu as pltpu
from jax.sharding import PartitionSpec as P

GAMMA = 5.0 / 3.0
COURANT = 0.12
LANES = 128
SUBS = 8
MESH = pl.DeviceIdType.MESH


def primitives(u):
    inverse = 1.0 / u[0]
    speeds = [u[1] * inverse, u[2] * inverse, u[3] * inverse]
    kinetic = 0.5 * (u[1] * speeds[0] + u[2] * speeds[1] + u[3] * speeds[2])
    pressure = (GAMMA - 1.0) * (u[4] - kinetic)
    square = GAMMA * pressure * inverse
    return speeds, pressure, square * lax.rsqrt(square)


def physical(u, prim, normal):
    speeds, pressure, sound = prim
    across = speeds[normal - 1]
    f = [u[normal], u[1] * across, u[2] * across, u[3] * across, (u[4] + pressure) * across]
    f[normal] = f[normal] + pressure
    return f, jnp.abs(across) + sound


def twice_flux(left, right):
    (ul, fl, sl), (ur, fr, sr) = left, right
    fastest = jnp.maximum(sl, sr)
    return [(a + b) - fastest * (d - c) for a, b, c, d in zip(fl, fr, ul, ur)]


def moved(u, f, s, normal, move):
    ud = [move(x) for x in u]
    fd = [ud[normal] if k == 0 else move(f[k]) for k in range(5)]
    return ud, fd, move(s)


def split_dot(x, table, terms):
    total = None
    for term in range(terms):
        part = x.astype(jnp.bfloat16)
        if term < terms - 1:
            x = x - part.astype(jnp.float32)
        add = jnp.dot(part, table, preferred_element_type=jnp.float32)
        total = add if total is None else total + add
    return total


def iota(shape, dim):
    return lax.broadcasted_iota(jnp.int32, shape, dim)


def lane_total(x):
    for shift in (1, 2, 4, 8, 16, 32, 64):
        x = x + pltpu.roll(x, shift, 1)
    return x


def kernel(
    dims,
    fine_hbm, coarse_hbm, neigh, csrc, cov,
    fine_out, coarse_out,
    fine, coarse, nxt_state, table, widened, rows_y, flux_d, restr, coarse_next,
    ids, req_send, req_recv, reqx_send, reqx_recv, rep_send, replies, rx_send, rx_recv,
    in_sem, out_sem, req_ss, req_rs, reqx_ss, reqx_rs, rep_ss, rep_rs, rx_ss, rx_rs,
):
    line, columns, gz_size, boxes, blocks, edge, half, slots = dims
    f32, i32 = jnp.float32, jnp.int32
    plane = edge * edge
    tiles = plane // LANES
    quarters = edge // SUBS
    faces = boxes * 6
    per_tile = LANES // edge
    gx = lax.axis_index("gx")
    gy = lax.axis_index("gy")
    gz = lax.axis_index("gz")
    me = gy * gz_size + gz

    def line_dev(p):
        return (gx, lax.div(p, gz_size), lax.rem(p, gz_size))

    def col_dev(x):
        return (x, gy, gz)

    load_fine = pltpu.make_async_copy(fine_hbm, fine, in_sem.at[0])
    load_coarse = pltpu.make_async_copy(coarse_hbm, coarse, in_sem.at[1])
    load_fine.start()
    load_coarse.start()

    barrier = pltpu.get_barrier_semaphore()
    for d in range(1, line):
        pl.semaphore_signal(barrier, 1, device_id=line_dev(lax.rem(me + d, line)), device_id_type=MESH)
    for d in range(1, columns):
        pl.semaphore_signal(barrier, 1, device_id=col_dev(lax.rem(gx + d, columns)), device_id_type=MESH)

    ids[...] = jnp.full((24, LANES), -1, i32)
    ids[0:boxes, 0:6] = neigh[...]
    ids[8 : 8 + boxes, 0:6] = csrc[...]
    ids[16:17, 0:blocks] = cov[...]
    lane8 = iota((SUBS, LANES), 1)
    sub8 = iota((SUBS, LANES), 0)

    def in_row(tile):
        row = tile[0:1, :]
        for b in range(1, boxes):
            lane1 = lane8[0:1, :]
            row = jnp.where(lane1 >= 6 * b, pltpu.roll(tile, 6 * b, 1)[b : b + 1, :], row)
        return jnp.broadcast_to(row, (line, LANES))

    lane = iota((line, LANES), 1)
    sub = iota((line, LANES), 0)
    near = in_row(ids[0:8, :])
    far = in_row(ids[8:16, :])
    is_fine = near >= 0
    near_dev = lax.div(near, jnp.full_like(near, boxes))
    far_dev = lax.div(far, jnp.full_like(far, blocks))
    side = lane
    for b in range(1, boxes):
        side = jnp.where(lane >= 6 * b, lane - 6 * b, side)
    facing = jnp.bitwise_xor(side, 1)
    code = jnp.where(
        is_fine,
        (near - near_dev * boxes) * 6 + facing,
        faces + (far - far_dev * blocks) * 6 + facing,
    )
    away = jnp.where(is_fine, near_dev, far_dev) - gx * line - me
    away = jnp.where(away < 0, away + line, away)
    match = (away == sub) & (lane < faces)
    ones = jnp.where(match, 1, 0)
    run = ones
    for shift in (1, 2, 4, 8):
        run = run + jnp.where(lane >= shift, pltpu.roll(run, shift, 1), 0)
    rank = run - ones
    asked = jnp.zeros((line, LANES), i32)
    for k in range(slots):
        asked = jnp.where(lane == k, lane_total(jnp.where(match & (rank == k), code, 0)), asked)
    for d in range(line):
        req_send[d] = jnp.broadcast_to(asked[d : d + 1, :], (SUBS, LANES))
    place = jnp.where(match & (rank < slots), sub * slots + rank, 0)
    place_tile = place[0:SUBS, :]
    for part in range(1, line // SUBS):
        place_tile = place_tile + place[part * SUBS : (part + 1) * SUBS, :]
    for shift in (1, 2, 4):
        place_tile = place_tile + pltpu.roll(place_tile, shift, 0)

    cover = jnp.broadcast_to(ids[16:17, :], (SUBS, LANES))
    cover_dev = lax.div(cover, jnp.full_like(cover, boxes))
    cover_col = lax.div(cover_dev, jnp.full_like(cover, line)) - gx
    cover_col = jnp.where(cover_col < 0, cover_col + columns, cover_col)
    covered = cover >= 0
    wanted = lane_total(
        jnp.where(covered & (cover_col == sub8), cover - cover_dev * boxes, 0)
    )
    for d in range(columns):
        reqx_send[d] = jnp.broadcast_to(wanted[d : d + 1, :], (SUBS, LANES))
    cover_col = jnp.where(covered, cover_col, 0)
    covered = jnp.where(covered, 1, 0)

    pl.semaphore_wait(barrier, line - 1 + columns - 1)

    req_copies = {}
    for d in range(1, line):
        req_copies[d] = pltpu.make_async_remote_copy(
            req_send.at[d], req_recv.at[d], req_ss.at[d], req_rs.at[d],
            device_id=line_dev(lax.rem(me + d, line)), device_id_type=MESH,
        )
        req_copies[d].start()
    reqx_copies = {}
    for d in range(1, columns):
        reqx_copies[d] = pltpu.make_async_remote_copy(
            reqx_send.at[d], reqx_recv.at[d], reqx_ss.at[d], reqx_rs.at[d],
            device_id=col_dev(lax.rem(gx + d, columns)), device_id_type=MESH,
        )
        reqx_copies[d].start()

    def tile_at(t):
        return pl.ds(t * LANES, LANES)

    in_edge = lane8 & (edge - 1)
    group = lane8 // edge
    load_fine.wait()

    def fine_layers(bc, carry):
        b = lax.div(bc, 5)
        c = bc - b * 5
        row = pl.multiple_of(bc * edge, edge)
        z_low = jnp.zeros((SUBS, LANES), f32)
        z_high = jnp.zeros((SUBS, LANES), f32)
        y_low = jnp.zeros((SUBS, LANES), f32)
        y_high = jnp.zeros((SUBS, LANES), f32)
        for q in range(quarters):
            for t in range(tiles):
                block = fine[pl.ds(row + q * SUBS, SUBS), tile_at(t)]
                s = q * SUBS + t
                z_low = jnp.where(in_edge == s, pltpu.roll(block, s, 1), z_low)
                z_high = jnp.where(in_edge == s, pltpu.roll(block, (s - edge + 1) % LANES, 1), z_high)
                if t == 0:
                    y_low = jnp.where(group == q, pltpu.roll(block, q * edge, 1), y_low)
                if t == tiles - 1:
                    y_high = jnp.where(
                        group == q, pltpu.roll(block, (q * edge - (LANES - edge)) % LANES, 1), y_high
                    )
                if q == 0:
                    table[b * 6, c, t : t + 1, :] = block[0:1, :]
                if q == quarters - 1:
                    table[b * 6 + 1, c, t : t + 1, :] = block[SUBS - 1 : SUBS, :]
        table[b * 6 + 2, c] = y_low
        table[b * 6 + 3, c] = y_high
        table[b * 6 + 4, c] = z_low
        table[b * 6 + 5, c] = z_high
        return carry

    lax.fori_loop(0, boxes * 5, fine_layers, 0)

    load_coarse.wait()
    small = half * half
    src = iota((small, 2 * LANES), 0)
    col = iota((small, 2 * LANES), 1)
    lane_w = col & (LANES - 1)
    y_src = (lane_w // edge) * ((half - 1) * half) + (lane_w & (edge - 1)) // 2
    z_j = 4 * (lane_w & (SUBS - 1)) + lane_w // edge
    z_src = (z_j // 2) * half + ((lane_w & (edge - 1)) // SUBS) * (half - 1)
    y_ok = (col < LANES) & (lane_w < 2 * edge) & (src == y_src)
    z_ok = (col >= LANES) & ((lane_w & (edge - 1)) < 2 * SUBS) & (src == z_src)
    lateral_table = jnp.where(y_ok | z_ok, 1.0, 0.0).astype(jnp.bfloat16)
    lateral = split_dot(coarse[...], lateral_table, 3)
    rows = blocks * 5 * half
    for part in range(2):
        piece = lateral[:, part * LANES : (part + 1) * LANES]
        widened[part, pl.ds(0, rows, stride=2), :] = piece
        widened[part, pl.ds(1, rows, stride=2), :] = piece
    z_group = in_edge // SUBS

    def coarse_layers(bc, carry):
        b = lax.div(bc, 5)
        c = bc - b * 5
        row = pl.multiple_of(bc * edge, edge)
        for f in range(2):
            y = jnp.zeros((SUBS, LANES), f32)
            z = jnp.zeros((SUBS, LANES), f32)
            for q in range(quarters):
                block = widened[0, pl.ds(row + q * SUBS, SUBS), :]
                y = jnp.where(group == q, pltpu.roll(block, (edge * (q - f)) % LANES, 1), y)
                block = widened[1, pl.ds(row + q * SUBS, SUBS), :]
                z = jnp.where(z_group == q, pltpu.roll(block, (SUBS * (q - f)) % LANES, 1), z)
            x = jnp.zeros((SUBS, LANES), f32)
            at = pl.multiple_of(bc * half, half)
            for t in range(SUBS):
                block = coarse[pl.ds(at + f * (half - SUBS), SUBS), tile_at(t // 4)]
                line_row = block[f * (SUBS - 1) : f * (SUBS - 1) + 1, :]
                line_row = jnp.broadcast_to(line_row, (SUBS, LANES))
                x = jnp.where(sub8 == t, pltpu.roll(line_row, (-2 * half * (t % 4)) % LANES, 1), x)
            rows_y[f, pl.ds(pl.multiple_of(bc * SUBS, SUBS), SUBS), :] = x
            table[faces + b * 6 + 2 + f, c] = y
            table[faces + b * 6 + 4 + f, c] = z
        return carry

    lax.fori_loop(0, blocks * 5, coarse_layers, 0)

    src = iota((LANES, LANES), 0)
    col = iota((LANES, LANES), 1)
    x_table = jnp.where(
        src == (col // (2 * edge)) * half + (col & (edge - 1)) // 2, 1.0, 0.0
    ).astype(jnp.bfloat16)
    for f in range(2):
        spread = split_dot(rows_y[f], x_table, 3)
        for b in range(blocks):
            for c in range(5):
                at = (b * 5 + c) * SUBS
                table[faces + b * 6 + f, c] = spread[at : at + SUBS, :]

    my_codes = asked[0:1, :]
    rep_copies = {}
    for d in list(range(1, line)) + [0]:
        if d:
            req_copies[d].wait_recv()
            codes = req_recv[d][0:1, :]
        else:
            codes = my_codes
        for k in range(slots):
            layer = table[codes[0, k]]
            if d:
                rep_send[d, k] = layer
            else:
                replies[d * slots + k] = layer
        if d:
            rep_copies[d] = pltpu.make_async_remote_copy(
                rep_send.at[d], replies.at[pl.ds(d * slots, slots)], rep_ss.at[d], rep_rs.at[d],
                device_id=line_dev(lax.rem(me + line - d, line)), device_id_type=MESH,
            )
            rep_copies[d].start()

    tall_lane = iota((edge, LANES), 1)
    tall_row = iota((edge, LANES), 0)
    not_last_x = tall_row < edge - 1
    not_last_z = (tall_lane & (edge - 1)) < edge - 1

    def box_step(b, carry):
        def load(t):
            return [
                fine[pl.ds(pl.multiple_of((b * 5 + c) * edge, edge), edge), tile_at(t)]
                for c in range(5)
            ]

        cur = load(0)
        prim = primitives(cur)
        before = [jnp.zeros((edge, LANES), f32)] * 5
        for t in range(tiles):
            if t < tiles - 1:
                after = load(t + 1)
                after_prim = primitives(after)
            else:
                after, after_prim = cur, prim
            f, s = physical(cur, prim, 1)
            right = moved(cur, f, s, 1, lambda x: pltpu.roll(x, edge - 1, 0))
            flux = [jnp.where(not_last_x, x, 0.0) for x in twice_flux((cur, f, s), right)]
            step = [x - pltpu.roll(x, 1, 0) for x in flux]
            f, s = physical(cur, prim, 3)
            right = moved(cur, f, s, 3, lambda x: pltpu.roll(x, LANES - 1, 1))
            flux = [jnp.where(not_last_z, x, 0.0) for x in twice_flux((cur, f, s), right)]
            step = [a + (x - pltpu.roll(x, 1, 1)) for a, x in zip(step, flux)]
            f, s = physical(cur, prim, 2)
            fa, sa = physical(after, after_prim, 2)

            def up(here, there):
                return pltpu.roll(jnp.where(tall_lane < edge, there, here), LANES - edge, 1)

            ud = [up(x, y) for x, y in zip(cur, after)]
            fd = [ud[2]] + [up(x, y) for x, y in zip(f[1:], fa[1:])]
            flux = twice_flux((cur, f, s), (ud, fd, up(s, sa)))
            if t == tiles - 1:
                flux = [jnp.where(tall_lane < LANES - edge, x, 0.0) for x in flux]
            for c in range(5):
                low = pltpu.roll(
                    jnp.where(tall_lane >= LANES - edge, before[c], flux[c]), edge, 1
                )
                total = step[c] + (flux[c] - low)
                nxt_state[t, pl.ds(pl.multiple_of((b * 5 + c) * edge, edge), edge), :] = (
                    cur[c] - (0.5 * COURANT) * total
                )
            before = flux
            cur, prim = after, after_prim
        return carry

    lax.fori_loop(0, boxes, box_step, 0)

    src = iota((4 * LANES, LANES), 0)
    col = iota((4 * LANES, LANES), 1)
    shrink = jnp.where(
        ((src // (2 * edge)) == col // half) & ((src & (edge - 1)) // 2 == (col & (half - 1))),
        0.125,
        0.0,
    ).astype(jnp.bfloat16)

    for d in range(1, line):
        rep_copies[d].wait_recv()
    for b in range(boxes):
        for g in range(6):
            ghost_all = replies[place_tile[0:1, :][0, b * 6 + g]]
            own_all = table[b * 6 + g]
            normal = g // 2 + 1
            pair = []
            for layers in (ghost_all, own_all):
                u = [layers[c] for c in range(5)]
                pair.append((u,) + physical(u, primitives(u), normal))
            if g % 2:
                flux = twice_flux(pair[1], pair[0])
                scale = -0.5 * COURANT
            else:
                flux = twice_flux(pair[0], pair[1])
                scale = 0.5 * COURANT
            for c in range(5):
                flux_d[b * 6 + g, c] = scale * flux[c]

    def add_faces(bc, carry):
        b = lax.div(bc, 5)
        c = bc - b * 5
        row = pl.multiple_of(bc * edge, edge)
        d = [flux_d[b * 6 + g, c] for g in range(6)]
        for q in range(quarters):
            for t in range(tiles):
                s = q * SUBS + t
                at = (t, pl.ds(row + q * SUBS, SUBS), slice(None))
                block = nxt_state[at]
                block = block + jnp.where(
                    in_edge == 0,
                    pltpu.roll(d[4], (-s) % LANES, 1),
                    jnp.where(in_edge == edge - 1, pltpu.roll(d[5], (edge - 1 - s) % LANES, 1), 0.0),
                )
                if t == 0:
                    block = block + jnp.where(group == 0, pltpu.roll(d[2], (-q * edge) % LANES, 1), 0.0)
                if t == tiles - 1:
                    block = block + jnp.where(
                        group == per_tile - 1,
                        pltpu.roll(d[3], (LANES - edge - q * edge) % LANES, 1),
                        0.0,
                    )
                if q == 0:
                    block = block + jnp.where(sub8 == 0, d[0][t : t + 1, :], 0.0)
                if q == quarters - 1:
                    block = block + jnp.where(sub8 == SUBS - 1, d[1][t : t + 1, :], 0.0)
                nxt_state[at] = block
        return carry

    lax.fori_loop(0, boxes * 5, add_faces, 0)

    stores = []
    for t in range(tiles):
        stores.append(
            pltpu.make_async_copy(nxt_state.at[t], fine_out.at[:, tile_at(t)], out_sem.at[1 + t])
        )
        stores[-1].start()

    for h in range(2):
        parts = []
        for t in range(4 * h, 4 * h + 4):
            parts.append(
                nxt_state[t, pl.ds(0, boxes * 5 * half, stride=2), :]
                + nxt_state[t, pl.ds(1, boxes * 5 * half, stride=2), :]
            )
        mean = split_dot(jnp.concatenate(parts, axis=1), shrink, 2)
        for b in range(boxes):
            restr[b, :, tile_at(h)] = mean[b * 5 * half : (b + 1) * 5 * half, :]

    rx_copies = {}
    for d in list(range(1, columns)) + [0]:
        if d:
            reqx_copies[d].wait_recv()
            which = reqx_recv[d][0:1, :][0, 0]
            rx_send[d] = restr[which]
            rx_copies[d] = pltpu.make_async_remote_copy(
                rx_send.at[d], rx_recv.at[d], rx_ss.at[d], rx_rs.at[d],
                device_id=col_dev(lax.rem(gx + columns - d, columns)), device_id_type=MESH,
            )
            rx_copies[d].start()
        else:
            rx_recv[0] = restr[wanted[0:1, :][0, 0]]
    for d in range(1, columns):
        rx_copies[d].wait_recv()
    for c in range(blocks):
        part = pl.ds(c * 5 * half, 5 * half)
        flag = covered[0:1, :][0, c]
        coarse_next[part, :] = jnp.where(flag > 0, rx_recv[cover_col[0:1, :][0, c]], coarse[part, :])
    store_coarse = pltpu.make_async_copy(coarse_next, coarse_out, out_sem.at[0])
    store_coarse.start()

    for copies in (req_copies, reqx_copies, rep_copies, rx_copies):
        for d in copies:
            copies[d].wait_send()
    for store in stores:
        store.wait()
    store_coarse.wait()


def body(fine_state, coarse_state, neighbours, coarse_sources, covering):
    boxes, comps, edge, plane = fine_state.shape
    blocks, _, half, small = coarse_state.shape
    line = lax.axis_size("gy") * lax.axis_size("gz")
    columns = lax.axis_size("gx")
    faces = boxes * 6
    slots = -(-faces // line)
    dims = (line, columns, lax.axis_size("gz"), boxes, blocks, edge, half, slots)
    fine_rows = boxes * comps * edge
    coarse_rows = blocks * comps * half
    f32, i32 = jnp.float32, jnp.int32
    vmem = pltpu.VMEM
    dma = pltpu.SemaphoreType.DMA
    layer = (comps, SUBS, LANES)
    fine_next, coarse_next = pl.pallas_call(
        functools.partial(kernel, dims),
        out_shape=(
            jax.ShapeDtypeStruct((fine_rows, plane), f32),
            jax.ShapeDtypeStruct((coarse_rows, small), f32),
        ),
        in_specs=[pl.BlockSpec(memory_space=pl.ANY)] * 2
        + [pl.BlockSpec(memory_space=pltpu.VMEM)] * 3,
        out_specs=(pl.BlockSpec(memory_space=pl.ANY),) * 2,
        scratch_shapes=[
            vmem((fine_rows, plane), f32),
            vmem((coarse_rows, small), f32),
            vmem((plane // LANES, fine_rows, LANES), f32),
            vmem((faces + 6 * blocks,) + layer, f32),
            vmem((2, 2 * coarse_rows, LANES), f32),
            vmem((2, blocks * comps * SUBS, LANES), f32),
            vmem((faces,) + layer, f32),
            vmem((boxes, comps * half, small), f32),
            vmem((coarse_rows, small), f32),
            vmem((24, LANES), i32),
            vmem((line, SUBS, LANES), i32),
            vmem((line, SUBS, LANES), i32),
            vmem((columns, SUBS, LANES), i32),
            vmem((columns, SUBS, LANES), i32),
            vmem((line, slots) + layer, f32),
            vmem((line * slots,) + layer, f32),
            vmem((columns, comps * half, small), f32),
            vmem((columns, comps * half, small), f32),
            dma((2,)),
            dma((1 + plane // LANES,)),
        ]
        + [dma((line,)), dma((line,)), dma((columns,)), dma((columns,))]
        + [dma((line,)), dma((line,)), dma((columns,)), dma((columns,))],
        compiler_params=pltpu.CompilerParams(
            collective_id=0, has_side_effects=True, vmem_limit_bytes=40 * 1024 * 1024
        ),
    )(
        fine_state.reshape(fine_rows, plane),
        coarse_state.reshape(coarse_rows, small),
        neighbours,
        coarse_sources,
        covering.reshape(1, blocks),
    )
    return fine_next.reshape(fine_state.shape), coarse_next.reshape(coarse_state.shape)


def solution(mesh):
    spec = ("gx", "gy", "gz")
    wide = P(spec, None, None, None)
    return jax.shard_map(
        body,
        mesh=mesh,
        in_specs=(wide, wide, P(spec, None), P(spec, None), P(spec)),
        out_specs=(wide, wide),
        check_vma=False,
    )
```

```python
import functools
import jax
import jax.numpy as jnp
from jax import lax
from jax.experimental import pallas as pl
from jax.experimental.pallas import tpu as pltpu
from jax.sharding import PartitionSpec as P

GAMMA = 5.0 / 3.0
COURANT = 0.12
LANES = 128
SUBS = 8
MESH = pl.DeviceIdType.MESH


def primitives(u):
    inverse = 1.0 / u[0]
    speeds = [u[1] * inverse, u[2] * inverse, u[3] * inverse]
    kinetic = 0.5 * (u[1] * speeds[0] + u[2] * speeds[1] + u[3] * speeds[2])
    pressure = (GAMMA - 1.0) * (u[4] - kinetic)
    square = GAMMA * pressure * inverse
    return speeds, pressure, square * lax.rsqrt(square)


def physical(u, prim, normal):
    speeds, pressure, sound = prim
    across = speeds[normal - 1]
    f = [u[normal], u[1] * across, u[2] * across, u[3] * across, (u[4] + pressure) * across]
    f[normal] = f[normal] + pressure
    return f, jnp.abs(across) + sound


def twice_flux(left, right):
    (ul, fl, sl), (ur, fr, sr) = left, right
    fastest = jnp.maximum(sl, sr)
    return [(a + b) - fastest * (d - c) for a, b, c, d in zip(fl, fr, ul, ur)]


def moved(u, f, s, normal, move):
    ud = [move(x) for x in u]
    fd = [ud[normal] if k == 0 else move(f[k]) for k in range(5)]
    return ud, fd, move(s)


def split_dot(x, table, terms):
    total = None
    for term in range(terms):
        part = x.astype(jnp.bfloat16)
        if term < terms - 1:
            x = x - part.astype(jnp.float32)
        add = jnp.dot(part, table, preferred_element_type=jnp.float32)
        total = add if total is None else total + add
    return total


def iota(shape, dim):
    return lax.broadcasted_iota(jnp.int32, shape, dim)


def lane_total(x):
    for shift in (1, 2, 4, 8, 16, 32, 64):
        x = x + pltpu.roll(x, shift, 1)
    return x


def kernel(
    dims,
    fine_hbm, coarse_hbm, neigh_hbm, csrc_hbm, cov_hbm,
    fine_out, coarse_out,
    fine, coarse, nxt_state, table, widened, rows_y, flux_d, restr, coarse_next,
    neigh, csrc, cov, ids, req_send, req_recv, reqx_send, reqx_recv, rep_send, replies, rx_send, rx_recv,
    in_sem, out_sem, req_ss, req_rs, reqx_ss, reqx_rs, rep_ss, rep_rs, rx_ss, rx_rs,
):
    line, columns, gz_size, boxes, blocks, edge, half, slots = dims
    f32, i32 = jnp.float32, jnp.int32
    plane = edge * edge
    tiles = plane // LANES
    quarters = edge // SUBS
    faces = boxes * 6
    per_tile = LANES // edge
    gx = lax.axis_index("gx")
    gy = lax.axis_index("gy")
    gz = lax.axis_index("gz")
    me = gy * gz_size + gz

    def line_dev(p):
        return (gx, lax.div(p, gz_size), lax.rem(p, gz_size))

    def col_dev(x):
        return (x, gy, gz)

    load_fine = pltpu.make_async_copy(fine_hbm, fine, in_sem.at[0])
    load_coarse = pltpu.make_async_copy(coarse_hbm, coarse, in_sem.at[1])
    load_ids = [
        pltpu.make_async_copy(a, b, in_sem.at[2 + i])
        for i, (a, b) in enumerate(((neigh_hbm, neigh), (csrc_hbm, csrc), (cov_hbm, cov)))
    ]
    for load in load_ids:
        load.start()
    load_fine.start()
    load_coarse.start()

    barrier = pltpu.get_barrier_semaphore()
    for d in range(1, line):
        pl.semaphore_signal(barrier, 1, device_id=line_dev(lax.rem(me + d, line)), device_id_type=MESH)
    for d in range(1, columns):
        pl.semaphore_signal(barrier, 1, device_id=col_dev(lax.rem(gx + d, columns)), device_id_type=MESH)

    for load in load_ids:
        load.wait()
    ids[...] = jnp.full((24, LANES), -1, i32)
    ids[0:boxes, 0:6] = neigh[...]
    ids[8 : 8 + boxes, 0:6] = csrc[...]
    ids[16:17, 0:blocks] = cov[...]
    lane8 = iota((SUBS, LANES), 1)
    sub8 = iota((SUBS, LANES), 0)

    def in_row(tile):
        row = tile[0:1, :]
        for b in range(1, boxes):
            lane1 = lane8[0:1, :]
            row = jnp.where(lane1 >= 6 * b, pltpu.roll(tile, 6 * b, 1)[b : b + 1, :], row)
        return jnp.broadcast_to(row, (line, LANES))

    lane = iota((line, LANES), 1)
    sub = iota((line, LANES), 0)
    near = in_row(ids[0:8, :])
    far = in_row(ids[8:16, :])
    is_fine = near >= 0
    near_dev = lax.div(near, jnp.full_like(near, boxes))
    far_dev = lax.div(far, jnp.full_like(far, blocks))
    side = lane
    for b in range(1, boxes):
        side = jnp.where(lane >= 6 * b, lane - 6 * b, side)
    facing = jnp.bitwise_xor(side, 1)
    code = jnp.where(
        is_fine,
        (near - near_dev * boxes) * 6 + facing,
        faces + (far - far_dev * blocks) * 6 + facing,
    )
    away = jnp.where(is_fine, near_dev, far_dev) - gx * line - me
    away = jnp.where(away < 0, away + line, away)
    match = (away == sub) & (lane < faces)
    ones = jnp.where(match, 1, 0)
    run = ones
    for shift in (1, 2, 4, 8):
        run = run + jnp.where(lane >= shift, pltpu.roll(run, shift, 1), 0)
    rank = run - ones
    asked = jnp.zeros((line, LANES), i32)
    for k in range(slots):
        asked = jnp.where(lane == k, lane_total(jnp.where(match & (rank == k), code, 0)), asked)
    for d in range(line):
        req_send[d] = jnp.broadcast_to(asked[d : d + 1, :], (SUBS, LANES))
    place = jnp.where(match & (rank < slots), sub * slots + rank, 0)
    place_tile = place[0:SUBS, :]
    for part in range(1, line // SUBS):
        place_tile = place_tile + place[part * SUBS : (part + 1) * SUBS, :]
    for shift in (1, 2, 4):
        place_tile = place_tile + pltpu.roll(place_tile, shift, 0)

    cover = jnp.broadcast_to(ids[16:17, :], (SUBS, LANES))
    cover_dev = lax.div(cover, jnp.full_like(cover, boxes))
    cover_col = lax.div(cover_dev, jnp.full_like(cover, line)) - gx
    cover_col = jnp.where(cover_col < 0, cover_col + columns, cover_col)
    covered = cover >= 0
    wanted = lane_total(
        jnp.where(covered & (cover_col == sub8), cover - cover_dev * boxes, 0)
    )
    for d in range(columns):
        reqx_send[d] = jnp.broadcast_to(wanted[d : d + 1, :], (SUBS, LANES))
    cover_col = jnp.where(covered, cover_col, 0)
    covered = jnp.where(covered, 1, 0)

    pl.semaphore_wait(barrier, line - 1 + columns - 1)

    req_copies = {}
    for d in range(1, line):
        req_copies[d] = pltpu.make_async_remote_copy(
            req_send.at[d], req_recv.at[d], req_ss.at[d], req_rs.at[d],
            device_id=line_dev(lax.rem(me + d, line)), device_id_type=MESH,
        )
        req_copies[d].start()
    reqx_copies = {}
    for d in range(1, columns):
        reqx_copies[d] = pltpu.make_async_remote_copy(
            reqx_send.at[d], reqx_recv.at[d], reqx_ss.at[d], reqx_rs.at[d],
            device_id=col_dev(lax.rem(gx + d, columns)), device_id_type=MESH,
        )
        reqx_copies[d].start()

    def tile_at(t):
        return pl.ds(t * LANES, LANES)

    in_edge = lane8 & (edge - 1)
    group = lane8 // edge
    load_fine.wait()

    def fine_layers(bc, carry):
        b = lax.div(bc, 5)
        c = bc - b * 5
        row = pl.multiple_of(bc * edge, edge)
        z_low = jnp.zeros((SUBS, LANES), f32)
        z_high = jnp.zeros((SUBS, LANES), f32)
        y_low = jnp.zeros((SUBS, LANES), f32)
        y_high = jnp.zeros((SUBS, LANES), f32)
        for q in range(quarters):
            for t in range(tiles):
                block = fine[pl.ds(row + q * SUBS, SUBS), tile_at(t)]
                s = q * SUBS + t
                z_low = jnp.where(in_edge == s, pltpu.roll(block, s, 1), z_low)
                z_high = jnp.where(in_edge == s, pltpu.roll(block, (s - edge + 1) % LANES, 1), z_high)
                if t == 0:
                    y_low = jnp.where(group == q, pltpu.roll(block, q * edge, 1), y_low)
                if t == tiles - 1:
                    y_high = jnp.where(
                        group == q, pltpu.roll(block, (q * edge - (LANES - edge)) % LANES, 1), y_high
                    )
                if q == 0:
                    table[b * 6, c, t : t + 1, :] = block[0:1, :]
                if q == quarters - 1:
                    table[b * 6 + 1, c, t : t + 1, :] = block[SUBS - 1 : SUBS, :]
        table[b * 6 + 2, c] = y_low
        table[b * 6 + 3, c] = y_high
        table[b * 6 + 4, c] = z_low
        table[b * 6 + 5, c] = z_high
        return carry

    lax.fori_loop(0, boxes * 5, fine_layers, 0)

    load_coarse.wait()
    small = half * half
    src = iota((small, 2 * LANES), 0)
    col = iota((small, 2 * LANES), 1)
    lane_w = col & (LANES - 1)
    y_src = (lane_w // edge) * ((half - 1) * half) + (lane_w & (edge - 1)) // 2
    z_j = 4 * (lane_w & (SUBS - 1)) + lane_w // edge
    z_src = (z_j // 2) * half + ((lane_w & (edge - 1)) // SUBS) * (half - 1)
    y_ok = (col < LANES) & (lane_w < 2 * edge) & (src == y_src)
    z_ok = (col >= LANES) & ((lane_w & (edge - 1)) < 2 * SUBS) & (src == z_src)
    lateral_table = jnp.where(y_ok | z_ok, 1.0, 0.0).astype(jnp.bfloat16)
    lateral = split_dot(coarse[...], lateral_table, 3)
    rows = blocks * 5 * half
    for part in range(2):
        piece = lateral[:, part * LANES : (part + 1) * LANES]
        widened[part, pl.ds(0, rows, stride=2), :] = piece
        widened[part, pl.ds(1, rows, stride=2), :] = piece
    z_group = in_edge // SUBS

    def coarse_layers(bc, carry):
        b = lax.div(bc, 5)
        c = bc - b * 5
        row = pl.multiple_of(bc * edge, edge)
        for f in range(2):
            y = jnp.zeros((SUBS, LANES), f32)
            z = jnp.zeros((SUBS, LANES), f32)
            for q in range(quarters):
                block = widened[0, pl.ds(row + q * SUBS, SUBS), :]
                y = jnp.where(group == q, pltpu.roll(block, (edge * (q - f)) % LANES, 1), y)
                block = widened[1, pl.ds(row + q * SUBS, SUBS), :]
                z = jnp.where(z_group == q, pltpu.roll(block, (SUBS * (q - f)) % LANES, 1), z)
            x = jnp.zeros((SUBS, LANES), f32)
            at = pl.multiple_of(bc * half, half)
            for t in range(SUBS):
                block = coarse[pl.ds(at + f * (half - SUBS), SUBS), tile_at(t // 4)]
                line_row = block[f * (SUBS - 1) : f * (SUBS - 1) + 1, :]
                line_row = jnp.broadcast_to(line_row, (SUBS, LANES))
                x = jnp.where(sub8 == t, pltpu.roll(line_row, (-2 * half * (t % 4)) % LANES, 1), x)
            rows_y[f, pl.ds(pl.multiple_of(bc * SUBS, SUBS), SUBS), :] = x
            table[faces + b * 6 + 2 + f, c] = y
            table[faces + b * 6 + 4 + f, c] = z
        return carry

    lax.fori_loop(0, blocks * 5, coarse_layers, 0)

    src = iota((LANES, LANES), 0)
    col = iota((LANES, LANES), 1)
    x_table = jnp.where(
        src == (col // (2 * edge)) * half + (col & (edge - 1)) // 2, 1.0, 0.0
    ).astype(jnp.bfloat16)
    for f in range(2):
        spread = split_dot(rows_y[f], x_table, 3)
        for b in range(blocks):
            for c in range(5):
                at = (b * 5 + c) * SUBS
                table[faces + b * 6 + f, c] = spread[at : at + SUBS, :]

    my_codes = asked[0:1, :]
    rep_copies = {}
    for d in list(range(1, line)) + [0]:
        if d:
            req_copies[d].wait_recv()
            codes = req_recv[d][0:1, :]
        else:
            codes = my_codes
        for k in range(slots):
            layer = table[codes[0, k]]
            if d:
                rep_send[d, k] = layer
            else:
                replies[d * slots + k] = layer
        if d:
            rep_copies[d] = pltpu.make_async_remote_copy(
                rep_send.at[d], replies.at[pl.ds(d * slots, slots)], rep_ss.at[d], rep_rs.at[d],
                device_id=line_dev(lax.rem(me + line - d, line)), device_id_type=MESH,
            )
            rep_copies[d].start()

    tall_lane = iota((edge, LANES), 1)
    tall_row = iota((edge, LANES), 0)
    not_last_x = tall_row < edge - 1
    not_last_z = (tall_lane & (edge - 1)) < edge - 1

    def box_step(b, carry):
        def load(t):
            return [
                fine[pl.ds(pl.multiple_of((b * 5 + c) * edge, edge), edge), tile_at(t)]
                for c in range(5)
            ]

        cur = load(0)
        prim = primitives(cur)
        before = [jnp.zeros((edge, LANES), f32)] * 5
        for t in range(tiles):
            if t < tiles - 1:
                after = load(t + 1)
                after_prim = primitives(after)
            else:
                after, after_prim = cur, prim
            f, s = physical(cur, prim, 1)
            right = moved(cur, f, s, 1, lambda x: pltpu.roll(x, edge - 1, 0))
            flux = [jnp.where(not_last_x, x, 0.0) for x in twice_flux((cur, f, s), right)]
            step = [x - pltpu.roll(x, 1, 0) for x in flux]
            f, s = physical(cur, prim, 3)
            right = moved(cur, f, s, 3, lambda x: pltpu.roll(x, LANES - 1, 1))
            flux = [jnp.where(not_last_z, x, 0.0) for x in twice_flux((cur, f, s), right)]
            step = [a + (x - pltpu.roll(x, 1, 1)) for a, x in zip(step, flux)]
            f, s = physical(cur, prim, 2)
            fa, sa = physical(after, after_prim, 2)

            def up(here, there):
                return pltpu.roll(jnp.where(tall_lane < edge, there, here), LANES - edge, 1)

            ud = [up(x, y) for x, y in zip(cur, after)]
            fd = [ud[2]] + [up(x, y) for x, y in zip(f[1:], fa[1:])]
            flux = twice_flux((cur, f, s), (ud, fd, up(s, sa)))
            if t == tiles - 1:
                flux = [jnp.where(tall_lane < LANES - edge, x, 0.0) for x in flux]
            for c in range(5):
                low = pltpu.roll(
                    jnp.where(tall_lane >= LANES - edge, before[c], flux[c]), edge, 1
                )
                total = step[c] + (flux[c] - low)
                nxt_state[t, pl.ds(pl.multiple_of((b * 5 + c) * edge, edge), edge), :] = (
                    cur[c] - (0.5 * COURANT) * total
                )
            before = flux
            cur, prim = after, after_prim
        return carry

    lax.fori_loop(0, boxes, box_step, 0)

    src = iota((4 * LANES, LANES), 0)
    col = iota((4 * LANES, LANES), 1)
    shrink = jnp.where(
        ((src // (2 * edge)) == col // half) & ((src & (edge - 1)) // 2 == (col & (half - 1))),
        0.125,
        0.0,
    ).astype(jnp.bfloat16)

    for d in range(1, line):
        rep_copies[d].wait_recv()
    for b in range(boxes):
        for g in range(6):
            ghost_all = replies[place_tile[0:1, :][0, b * 6 + g]]
            own_all = table[b * 6 + g]
            normal = g // 2 + 1
            pair = []
            for layers in (ghost_all, own_all):
                u = [layers[c] for c in range(5)]
                pair.append((u,) + physical(u, primitives(u), normal))
            if g % 2:
                flux = twice_flux(pair[1], pair[0])
                scale = -0.5 * COURANT
            else:
                flux = twice_flux(pair[0], pair[1])
                scale = 0.5 * COURANT
            for c in range(5):
                flux_d[b * 6 + g, c] = scale * flux[c]

    def add_faces(bc, carry):
        b = lax.div(bc, 5)
        c = bc - b * 5
        row = pl.multiple_of(bc * edge, edge)
        d = [flux_d[b * 6 + g, c] for g in range(6)]
        for q in range(quarters):
            for t in range(tiles):
                s = q * SUBS + t
                at = (t, pl.ds(row + q * SUBS, SUBS), slice(None))
                block = nxt_state[at]
                block = block + jnp.where(
                    in_edge == 0,
                    pltpu.roll(d[4], (-s) % LANES, 1),
                    jnp.where(in_edge == edge - 1, pltpu.roll(d[5], (edge - 1 - s) % LANES, 1), 0.0),
                )
                if t == 0:
                    block = block + jnp.where(group == 0, pltpu.roll(d[2], (-q * edge) % LANES, 1), 0.0)
                if t == tiles - 1:
                    block = block + jnp.where(
                        group == per_tile - 1,
                        pltpu.roll(d[3], (LANES - edge - q * edge) % LANES, 1),
                        0.0,
                    )
                if q == 0:
                    block = block + jnp.where(sub8 == 0, d[0][t : t + 1, :], 0.0)
                if q == quarters - 1:
                    block = block + jnp.where(sub8 == SUBS - 1, d[1][t : t + 1, :], 0.0)
                nxt_state[at] = block
        return carry

    lax.fori_loop(0, boxes * 5, add_faces, 0)

    stores = []
    for t in range(tiles):
        stores.append(
            pltpu.make_async_copy(nxt_state.at[t], fine_out.at[:, tile_at(t)], out_sem.at[1 + t])
        )
        stores[-1].start()

    for h in range(2):
        parts = []
        for t in range(4 * h, 4 * h + 4):
            parts.append(
                nxt_state[t, pl.ds(0, boxes * 5 * half, stride=2), :]
                + nxt_state[t, pl.ds(1, boxes * 5 * half, stride=2), :]
            )
        mean = split_dot(jnp.concatenate(parts, axis=1), shrink, 2)
        for b in range(boxes):
            restr[b, :, tile_at(h)] = mean[b * 5 * half : (b + 1) * 5 * half, :]

    rx_copies = {}
    for d in list(range(1, columns)) + [0]:
        if d:
            reqx_copies[d].wait_recv()
            which = reqx_recv[d][0:1, :][0, 0]
            rx_send[d] = restr[which]
            rx_copies[d] = pltpu.make_async_remote_copy(
                rx_send.at[d], rx_recv.at[d], rx_ss.at[d], rx_rs.at[d],
                device_id=col_dev(lax.rem(gx + columns - d, columns)), device_id_type=MESH,
            )
            rx_copies[d].start()
        else:
            rx_recv[0] = restr[wanted[0:1, :][0, 0]]
    for d in range(1, columns):
        rx_copies[d].wait_recv()
    for c in range(blocks):
        part = pl.ds(c * 5 * half, 5 * half)
        flag = covered[0:1, :][0, c]
        coarse_next[part, :] = jnp.where(flag > 0, rx_recv[cover_col[0:1, :][0, c]], coarse[part, :])
    store_coarse = pltpu.make_async_copy(coarse_next, coarse_out, out_sem.at[0])
    store_coarse.start()

    for copies in (req_copies, reqx_copies, rep_copies, rx_copies):
        for d in copies:
            copies[d].wait_send()
    for store in stores:
        store.wait()
    store_coarse.wait()


def body(fine_state, coarse_state, neighbours, coarse_sources, covering):
    boxes, comps, edge, plane = fine_state.shape
    blocks, _, half, small = coarse_state.shape
    line = lax.axis_size("gy") * lax.axis_size("gz")
    columns = lax.axis_size("gx")
    faces = boxes * 6
    slots = -(-faces // line)
    dims = (line, columns, lax.axis_size("gz"), boxes, blocks, edge, half, slots)
    fine_rows = boxes * comps * edge
    coarse_rows = blocks * comps * half
    f32, i32 = jnp.float32, jnp.int32
    vmem = pltpu.VMEM
    dma = pltpu.SemaphoreType.DMA
    layer = (comps, SUBS, LANES)
    fine_next, coarse_next = pl.pallas_call(
        functools.partial(kernel, dims),
        out_shape=(
            jax.ShapeDtypeStruct((fine_rows, plane), f32),
            jax.ShapeDtypeStruct((coarse_rows, small), f32),
        ),
        in_specs=[pl.BlockSpec(memory_space=pl.ANY)] * 5,
        out_specs=(pl.BlockSpec(memory_space=pl.ANY),) * 2,
        scratch_shapes=[
            vmem((fine_rows, plane), f32),
            vmem((coarse_rows, small), f32),
            vmem((plane // LANES, fine_rows, LANES), f32),
            vmem((faces + 6 * blocks,) + layer, f32),
            vmem((2, 2 * coarse_rows, LANES), f32),
            vmem((2, blocks * comps * SUBS, LANES), f32),
            vmem((faces,) + layer, f32),
            vmem((boxes, comps * half, small), f32),
            vmem((coarse_rows, small), f32),
            vmem((boxes, 6), i32),
            vmem((boxes, 6), i32),
            vmem((1, blocks), i32),
            vmem((24, LANES), i32),
            vmem((line, SUBS, LANES), i32),
            vmem((line, SUBS, LANES), i32),
            vmem((columns, SUBS, LANES), i32),
            vmem((columns, SUBS, LANES), i32),
            vmem((line, slots) + layer, f32),
            vmem((line * slots,) + layer, f32),
            vmem((columns, comps * half, small), f32),
            vmem((columns, comps * half, small), f32),
            dma((5,)),
            dma((1 + plane // LANES,)),
        ]
        + [dma((line,)), dma((line,)), dma((columns,)), dma((columns,))]
        + [dma((line,)), dma((line,)), dma((columns,)), dma((columns,))],
        compiler_params=pltpu.CompilerParams(
            collective_id=0, has_side_effects=True, vmem_limit_bytes=62 * 1024 * 1024
        ),
    )(
        fine_state.reshape(fine_rows, plane),
        coarse_state.reshape(coarse_rows, small),
        neighbours,
        coarse_sources,
        covering.reshape(1, blocks),
    )
    return fine_next.reshape(fine_state.shape), coarse_next.reshape(coarse_state.shape)


def solution(mesh):
    spec = ("gx", "gy", "gz")
    wide = P(spec, None, None, None)
    return jax.shard_map(
        body,
        mesh=mesh,
        in_specs=(wide, wide, P(spec, None), P(spec, None), P(spec)),
        out_specs=(wide, wide),
        check_vma=False,
    )
```

```python
import functools
import jax
import jax.numpy as jnp
from jax import lax
from jax.experimental import pallas as pl
from jax.experimental.pallas import tpu as pltpu
from jax.sharding import PartitionSpec as P

GAMMA = 5.0 / 3.0
COURANT = 0.12
LANES = 128
SUBS = 8
MESH = pl.DeviceIdType.MESH


def primitives(u):
    inverse = 1.0 / u[0]
    speeds = [u[1] * inverse, u[2] * inverse, u[3] * inverse]
    kinetic = 0.5 * (u[1] * speeds[0] + u[2] * speeds[1] + u[3] * speeds[2])
    pressure = (GAMMA - 1.0) * (u[4] - kinetic)
    square = GAMMA * pressure * inverse
    return speeds, pressure, square * lax.rsqrt(square)


def physical(u, prim, normal):
    speeds, pressure, sound = prim
    across = speeds[normal - 1]
    f = [u[normal], u[1] * across, u[2] * across, u[3] * across, (u[4] + pressure) * across]
    f[normal] = f[normal] + pressure
    return f, jnp.abs(across) + sound


def twice_flux(left, right):
    (ul, fl, sl), (ur, fr, sr) = left, right
    fastest = jnp.maximum(sl, sr)
    return [(a + b) - fastest * (d - c) for a, b, c, d in zip(fl, fr, ul, ur)]


def moved(u, f, s, normal, move):
    ud = [move(x) for x in u]
    fd = [ud[normal] if k == 0 else move(f[k]) for k in range(5)]
    return ud, fd, move(s)


def split_dot(x, table, terms):
    total = None
    for term in range(terms):
        part = x.astype(jnp.bfloat16)
        if term < terms - 1:
            x = x - part.astype(jnp.float32)
        add = jnp.dot(part, table, preferred_element_type=jnp.float32)
        total = add if total is None else total + add
    return total


def iota(shape, dim):
    return lax.broadcasted_iota(jnp.int32, shape, dim)


def lane_total(x):
    for shift in (1, 2, 4, 8, 16, 32, 64):
        x = x + pltpu.roll(x, shift, 1)
    return x


def kernel(
    dims,
    fine_hbm, coarse_hbm, neigh_hbm, csrc_hbm, cov_hbm,
    fine_out, coarse_out,
    fine, coarse, nxt_state, table, widened, rows_y, flux_d, restr, coarse_next,
    neigh, csrc, cov, ids, req_send, req_recv, reqx_send, reqx_recv, rep_send, replies, rx_send, rx_recv,
    carried, pooled, pool_send, pool_recv,
    in_sem, out_sem, req_ss, req_rs, reqx_ss, reqx_rs, rep_ss, rep_rs, rx_ss, rx_rs,
):
    line, columns, gz_size, boxes, blocks, edge, half, slots = dims
    f32, i32 = jnp.float32, jnp.int32
    plane = edge * edge
    tiles = plane // LANES
    quarters = edge // SUBS
    faces = boxes * 6
    per_tile = LANES // edge
    gx = lax.axis_index("gx")
    gy = lax.axis_index("gy")
    gz = lax.axis_index("gz")
    me = gy * gz_size + gz

    def line_dev(p):
        return (gx, lax.div(p, gz_size), lax.rem(p, gz_size))

    def col_dev(x):
        return (x, gy, gz)

    load_fine = pltpu.make_async_copy(fine_hbm, fine, in_sem.at[0])
    load_coarse = pltpu.make_async_copy(coarse_hbm, coarse, in_sem.at[1])
    load_ids = [
        pltpu.make_async_copy(a, b, in_sem.at[2 + i])
        for i, (a, b) in enumerate(((neigh_hbm, neigh), (csrc_hbm, csrc), (cov_hbm, cov)))
    ]
    for load in load_ids:
        load.start()
    load_fine.start()
    load_coarse.start()

    barrier = pltpu.get_barrier_semaphore()
    for d in range(1, line):
        pl.semaphore_signal(barrier, 1, device_id=line_dev(lax.rem(me + d, line)), device_id_type=MESH)
    for d in range(1, columns):
        pl.semaphore_signal(barrier, 1, device_id=col_dev(lax.rem(gx + d, columns)), device_id_type=MESH)

    for load in load_ids:
        load.wait()
    ids[...] = jnp.full((24, LANES), -1, i32)
    ids[0:boxes, 0:6] = neigh[...]
    ids[8 : 8 + boxes, 0:6] = csrc[...]
    ids[16:17, 0:blocks] = cov[...]
    lane8 = iota((SUBS, LANES), 1)
    sub8 = iota((SUBS, LANES), 0)

    def in_row(tile):
        row = tile[0:1, :]
        for b in range(1, boxes):
            lane1 = lane8[0:1, :]
            row = jnp.where(lane1 >= 6 * b, pltpu.roll(tile, 6 * b, 1)[b : b + 1, :], row)
        return jnp.broadcast_to(row, (line, LANES))

    lane = iota((line, LANES), 1)
    sub = iota((line, LANES), 0)
    near = in_row(ids[0:8, :])
    far = in_row(ids[8:16, :])
    is_fine = near >= 0
    near_dev = lax.div(near, jnp.full_like(near, boxes))
    far_dev = lax.div(far, jnp.full_like(far, blocks))
    side = lane
    for b in range(1, boxes):
        side = jnp.where(lane >= 6 * b, lane - 6 * b, side)
    facing = jnp.bitwise_xor(side, 1)
    code = jnp.where(
        is_fine,
        (near - near_dev * boxes) * 6 + facing,
        faces + (far - far_dev * blocks) * 6 + facing,
    )
    away = jnp.where(is_fine, near_dev, far_dev) - gx * line - me
    away = jnp.where(away < 0, away + line, away)
    match = (away == sub) & (lane < faces)
    ones = jnp.where(match, 1, 0)
    run = ones
    for shift in (1, 2, 4, 8):
        run = run + jnp.where(lane >= shift, pltpu.roll(run, shift, 1), 0)
    rank = run - ones
    asked = jnp.zeros((line, LANES), i32)
    for k in range(slots):
        asked = jnp.where(lane == k, lane_total(jnp.where(match & (rank == k), code, 0)), asked)
    for d in range(line):
        req_send[d] = jnp.broadcast_to(asked[d : d + 1, :], (SUBS, LANES))
    place = jnp.where(match & (rank < slots), sub * slots + rank, 0)
    place_tile = place[0:SUBS, :]
    for part in range(1, line // SUBS):
        place_tile = place_tile + place[part * SUBS : (part + 1) * SUBS, :]
    for shift in (1, 2, 4):
        place_tile = place_tile + pltpu.roll(place_tile, shift, 0)

    cover = jnp.broadcast_to(ids[16:17, :], (SUBS, LANES))
    cover_dev = lax.div(cover, jnp.full_like(cover, boxes))
    cover_col = lax.div(cover_dev, jnp.full_like(cover, line)) - gx
    cover_col = jnp.where(cover_col < 0, cover_col + columns, cover_col)
    covered = cover >= 0
    wanted = lane_total(
        jnp.where(covered & (cover_col == sub8), cover - cover_dev * boxes, 0)
    )
    for d in range(columns):
        reqx_send[d] = jnp.broadcast_to(wanted[d : d + 1, :], (SUBS, LANES))
    cover_col = jnp.where(covered, cover_col, 0)
    covered = jnp.where(covered, 1, 0)

    pl.semaphore_wait(barrier, line - 1 + columns - 1)

    req_copies = {}
    for d in range(1, line):
        req_copies[d] = pltpu.make_async_remote_copy(
            req_send.at[d], req_recv.at[d], req_ss.at[d], req_rs.at[d],
            device_id=line_dev(lax.rem(me + d, line)), device_id_type=MESH,
        )
        req_copies[d].start()
    reqx_copies = {}
    for d in range(1, columns):
        reqx_copies[d] = pltpu.make_async_remote_copy(
            reqx_send.at[d], reqx_recv.at[d], reqx_ss.at[d], reqx_rs.at[d],
            device_id=col_dev(lax.rem(gx + d, columns)), device_id_type=MESH,
        )
        reqx_copies[d].start()

    def tile_at(t):
        return pl.ds(t * LANES, LANES)

    in_edge = lane8 & (edge - 1)
    group = lane8 // edge
    load_fine.wait()

    def fine_layers(bc, carry):
        b = lax.div(bc, 5)
        c = bc - b * 5
        row = pl.multiple_of(bc * edge, edge)
        z_low = jnp.zeros((SUBS, LANES), f32)
        z_high = jnp.zeros((SUBS, LANES), f32)
        y_low = jnp.zeros((SUBS, LANES), f32)
        y_high = jnp.zeros((SUBS, LANES), f32)
        for q in range(quarters):
            for t in range(tiles):
                block = fine[pl.ds(row + q * SUBS, SUBS), tile_at(t)]
                s = q * SUBS + t
                z_low = jnp.where(in_edge == s, pltpu.roll(block, s, 1), z_low)
                z_high = jnp.where(in_edge == s, pltpu.roll(block, (s - edge + 1) % LANES, 1), z_high)
                if t == 0:
                    y_low = jnp.where(group == q, pltpu.roll(block, q * edge, 1), y_low)
                if t == tiles - 1:
                    y_high = jnp.where(
                        group == q, pltpu.roll(block, (q * edge - (LANES - edge)) % LANES, 1), y_high
                    )
                if q == 0:
                    table[b * 6, c, t : t + 1, :] = block[0:1, :]
                if q == quarters - 1:
                    table[b * 6 + 1, c, t : t + 1, :] = block[SUBS - 1 : SUBS, :]
        table[b * 6 + 2, c] = y_low
        table[b * 6 + 3, c] = y_high
        table[b * 6 + 4, c] = z_low
        table[b * 6 + 5, c] = z_high
        return carry

    lax.fori_loop(0, boxes * 5, fine_layers, 0)

    load_coarse.wait()
    small = half * half
    src = iota((small, 2 * LANES), 0)
    col = iota((small, 2 * LANES), 1)
    lane_w = col & (LANES - 1)
    y_src = (lane_w // edge) * ((half - 1) * half) + (lane_w & (edge - 1)) // 2
    z_j = 4 * (lane_w & (SUBS - 1)) + lane_w // edge
    z_src = (z_j // 2) * half + ((lane_w & (edge - 1)) // SUBS) * (half - 1)
    y_ok = (col < LANES) & (lane_w < 2 * edge) & (src == y_src)
    z_ok = (col >= LANES) & ((lane_w & (edge - 1)) < 2 * SUBS) & (src == z_src)
    lateral_table = jnp.where(y_ok | z_ok, 1.0, 0.0).astype(jnp.bfloat16)
    lateral = split_dot(coarse[...], lateral_table, 3)
    rows = blocks * 5 * half
    for part in range(2):
        piece = lateral[:, part * LANES : (part + 1) * LANES]
        widened[part, pl.ds(0, rows, stride=2), :] = piece
        widened[part, pl.ds(1, rows, stride=2), :] = piece
    z_group = in_edge // SUBS

    def coarse_layers(bc, carry):
        b = lax.div(bc, 5)
        c = bc - b * 5
        row = pl.multiple_of(bc * edge, edge)
        for f in range(2):
            y = jnp.zeros((SUBS, LANES), f32)
            z = jnp.zeros((SUBS, LANES), f32)
            for q in range(quarters):
                block = widened[0, pl.ds(row + q * SUBS, SUBS), :]
                y = jnp.where(group == q, pltpu.roll(block, (edge * (q - f)) % LANES, 1), y)
                block = widened[1, pl.ds(row + q * SUBS, SUBS), :]
                z = jnp.where(z_group == q, pltpu.roll(block, (SUBS * (q - f)) % LANES, 1), z)
            x = jnp.zeros((SUBS, LANES), f32)
            at = pl.multiple_of(bc * half, half)
            for t in range(SUBS):
                block = coarse[pl.ds(at + f * (half - SUBS), SUBS), tile_at(t // 4)]
                line_row = block[f * (SUBS - 1) : f * (SUBS - 1) + 1, :]
                line_row = jnp.broadcast_to(line_row, (SUBS, LANES))
                x = jnp.where(sub8 == t, pltpu.roll(line_row, (-2 * half * (t % 4)) % LANES, 1), x)
            rows_y[f, pl.ds(pl.multiple_of(bc * SUBS, SUBS), SUBS), :] = x
            table[faces + b * 6 + 2 + f, c] = y
            table[faces + b * 6 + 4 + f, c] = z
        return carry

    lax.fori_loop(0, blocks * 5, coarse_layers, 0)

    src = iota((LANES, LANES), 0)
    col = iota((LANES, LANES), 1)
    x_table = jnp.where(
        src == (col // (2 * edge)) * half + (col & (edge - 1)) // 2, 1.0, 0.0
    ).astype(jnp.bfloat16)
    for f in range(2):
        spread = split_dot(rows_y[f], x_table, 3)
        for b in range(blocks):
            for c in range(5):
                at = (b * 5 + c) * SUBS
                table[faces + b * 6 + f, c] = spread[at : at + SUBS, :]

    my_codes = asked[0:1, :]
    rep_copies = {}
    for d in list(range(1, line)) + [0]:
        if d:
            req_copies[d].wait_recv()
            codes = req_recv[d][0:1, :]
        else:
            codes = my_codes
        for k in range(slots):
            layer = table[codes[0, k]]
            if d:
                rep_send[d, k] = layer
            else:
                replies[d * slots + k] = layer
        if d:
            rep_copies[d] = pltpu.make_async_remote_copy(
                rep_send.at[d], replies.at[pl.ds(d * slots, slots)], rep_ss.at[d], rep_rs.at[d],
                device_id=line_dev(lax.rem(me + line - d, line)), device_id_type=MESH,
            )
            rep_copies[d].start()

    src = iota((4 * LANES, LANES), 0)
    col = iota((4 * LANES, LANES), 1)
    shrink = jnp.where(
        ((src // (2 * edge)) == col // half) & ((src & (edge - 1)) // 2 == (col & (half - 1))),
        0.125,
        0.0,
    ).astype(jnp.bfloat16)

    tall_lane = iota((edge, LANES), 1)
    tall_row = iota((edge, LANES), 0)
    not_last_x = tall_row < edge - 1
    not_last_z = (tall_lane & (edge - 1)) < edge - 1

    def box_step(half_box, b):
        def load(t):
            return [
                fine[pl.ds(pl.multiple_of((b * 5 + c) * edge, edge), edge), tile_at(t)]
                for c in range(5)
            ]

        first = half_box * (tiles // 2)
        cur = load(first)
        prim = primitives(cur)
        if half_box:
            before = [carried[b, c] for c in range(5)]
        else:
            before = [jnp.zeros((edge, LANES), f32)] * 5
        for t in range(first, first + tiles // 2):
            if t < tiles - 1:
                after = load(t + 1)
                after_prim = primitives(after)
            else:
                after, after_prim = cur, prim
            f, s = physical(cur, prim, 1)
            right = moved(cur, f, s, 1, lambda x: pltpu.roll(x, edge - 1, 0))
            flux = [jnp.where(not_last_x, x, 0.0) for x in twice_flux((cur, f, s), right)]
            step = [x - pltpu.roll(x, 1, 0) for x in flux]
            f, s = physical(cur, prim, 3)
            right = moved(cur, f, s, 3, lambda x: pltpu.roll(x, LANES - 1, 1))
            flux = [jnp.where(not_last_z, x, 0.0) for x in twice_flux((cur, f, s), right)]
            step = [a + (x - pltpu.roll(x, 1, 1)) for a, x in zip(step, flux)]
            f, s = physical(cur, prim, 2)
            fa, sa = physical(after, after_prim, 2)

            def up(here, there):
                return pltpu.roll(jnp.where(tall_lane < edge, there, here), LANES - edge, 1)

            ud = [up(x, y) for x, y in zip(cur, after)]
            fd = [ud[2]] + [up(x, y) for x, y in zip(f[1:], fa[1:])]
            flux = twice_flux((cur, f, s), (ud, fd, up(s, sa)))
            if t == tiles - 1:
                flux = [jnp.where(tall_lane < LANES - edge, x, 0.0) for x in flux]
            for c in range(5):
                low = pltpu.roll(
                    jnp.where(tall_lane >= LANES - edge, before[c], flux[c]), edge, 1
                )
                total = step[c] + (flux[c] - low)
                nxt_state[t, pl.ds(pl.multiple_of((b * 5 + c) * edge, edge), edge), :] = (
                    cur[c] - (0.5 * COURANT) * total
                )
            before = flux
            cur, prim = after, after_prim
        if not half_box:
            for c in range(5):
                carried[b, c] = before[c]

    pairs = 5 * half
    rx_copies = {}
    for h in range(2):

        def one_box(b, carry):
            box_step(h, b)
            start = b * 5 * edge
            parts = [
                nxt_state[t, pl.ds(start, pairs, stride=2), :]
                + nxt_state[t, pl.ds(start + 1, pairs, stride=2), :]
                for t in range(4 * h, 4 * h + 4)
            ]
            restr[b, h] = split_dot(jnp.concatenate(parts, axis=1), shrink, 2)
            return carry

        lax.fori_loop(0, boxes, one_box, 0)
        for d in range(columns):
            if d and not h:
                reqx_copies[d].wait_recv()
            if d:
                rx_send[d, h] = restr[reqx_recv[d][0:1, :][0, 0], h]
                rx_copies[d, h] = pltpu.make_async_remote_copy(
                    rx_send.at[d, h], rx_recv.at[d, h], rx_ss.at[d * 3 + h], rx_rs.at[d * 3 + h],
                    device_id=col_dev(lax.rem(gx + columns - d, columns)), device_id_type=MESH,
                )
                rx_copies[d, h].start()
            else:
                rx_recv[d, h] = restr[wanted[0:1, :][0, 0], h]

    src = iota((2 * LANES, LANES), 0)
    col = iota((2 * LANES, LANES), 1)
    upper = src // LANES
    src = src & (LANES - 1)
    src_t = src & (SUBS - 1)
    src_q = (src & (edge - 1)) // SUBS
    to_z = ((src_t & 3) * 2 + src // (2 * edge)) * half + upper * SUBS + (src_t // 4) * 4 + src_q
    to_y = upper * (LANES // 2) + src // 2
    pool_z = jnp.where(col == to_z, 0.125, 0.0).astype(jnp.bfloat16)
    pool_y = jnp.where(col == to_y, 0.125, 0.0).astype(jnp.bfloat16)

    for d in range(1, line):
        rep_copies[d].wait_recv()
    for b in range(boxes):
        for g in range(6):
            ghost_all = replies[place_tile[0:1, :][0, b * 6 + g]]
            own_all = table[b * 6 + g]
            normal = g // 2 + 1
            pair = []
            for layers in (ghost_all, own_all):
                u = [layers[c] for c in range(5)]
                pair.append((u,) + physical(u, primitives(u), normal))
            if g % 2:
                flux = twice_flux(pair[1], pair[0])
                scale = -0.5 * COURANT
            else:
                flux = twice_flux(pair[0], pair[1])
                scale = 0.5 * COURANT
            for c in range(5):
                flux_d[pl.ds(((b * 6 + g) * 5 + c) * SUBS, SUBS), :] = scale * flux[c]

    for b in range(boxes):
        at = b * 6 * 5 * SUBS
        parts = [flux_d[pl.ds(at + e, 20, stride=4), :] for e in range(4)]
        pooled[b, 0:20, :] = split_dot(jnp.concatenate(parts, axis=1), shrink, 2)
        for g, pool in ((2, pool_y), (4, pool_z)):
            parts = []
            for f in (g, g + 1):
                at = (b * 6 + f) * 5 * SUBS
                parts.append(flux_d[pl.ds(at, 20, stride=2), :] + flux_d[pl.ds(at + 1, 20, stride=2), :])
            pooled[b, 10 * g : 10 * g + 20, :] = split_dot(jnp.concatenate(parts, axis=1), pool, 2)
        pooled[b, 60:64, :] = jnp.zeros((4, LANES), f32)
    for d in range(columns):
        if d:
            pool_send[d] = pooled[reqx_recv[d][0:1, :][0, 0]]
            rx_copies[d, 2] = pltpu.make_async_remote_copy(
                pool_send.at[d], pool_recv.at[d], rx_ss.at[d * 3 + 2], rx_rs.at[d * 3 + 2],
                device_id=col_dev(lax.rem(gx + columns - d, columns)), device_id_type=MESH,
            )
            rx_copies[d, 2].start()
        else:
            pool_recv[d] = pooled[wanted[0:1, :][0, 0]]

    def add_faces(bc, carry):
        b = lax.div(bc, 5)
        c = bc - b * 5
        row = pl.multiple_of(bc * edge, edge)
        d = [
            flux_d[pl.ds(pl.multiple_of(((b * 6 + g) * 5 + c) * SUBS, SUBS), SUBS), :]
            for g in range(6)
        ]
        for q in range(quarters):
            for t in range(tiles):
                s = q * SUBS + t
                at = (t, pl.ds(row + q * SUBS, SUBS), slice(None))
                block = nxt_state[at]
                block = block + jnp.where(
                    in_edge == 0,
                    pltpu.roll(d[4], (-s) % LANES, 1),
                    jnp.where(in_edge == edge - 1, pltpu.roll(d[5], (edge - 1 - s) % LANES, 1), 0.0),
                )
                if t == 0:
                    block = block + jnp.where(group == 0, pltpu.roll(d[2], (-q * edge) % LANES, 1), 0.0)
                if t == tiles - 1:
                    block = block + jnp.where(
                        group == per_tile - 1,
                        pltpu.roll(d[3], (LANES - edge - q * edge) % LANES, 1),
                        0.0,
                    )
                if q == 0:
                    block = block + jnp.where(sub8 == 0, d[0][t : t + 1, :], 0.0)
                if q == quarters - 1:
                    block = block + jnp.where(sub8 == SUBS - 1, d[1][t : t + 1, :], 0.0)
                nxt_state[at] = block
        return carry

    lax.fori_loop(0, boxes * 5, add_faces, 0)

    stores = []
    for t in range(tiles):
        stores.append(
            pltpu.make_async_copy(nxt_state.at[t], fine_out.at[:, tile_at(t)], out_sem.at[1 + t])
        )
        stores[-1].start()

    wide20 = iota((20, LANES), 1)
    low_z = (wide20 & (half - 1)) == 0
    high_z = (wide20 & (half - 1)) == half - 1
    low_y = wide20 < half
    high_y = wide20 >= LANES - half
    for d in range(columns):
        if d:
            for h in range(3):
                rx_copies[d, h].wait_recv()
        x, y, z = (pool_recv[d, pl.ds(20 * i, 20), :] for i in range(3))
        for q in range(quarters):
            for h in range(2):
                s = h * 4 + q
                add = jnp.where(
                    low_z,
                    pltpu.roll(z, (-s) % LANES, 1),
                    jnp.where(high_z, pltpu.roll(z, (half - 1 - SUBS - s) % LANES, 1), 0.0),
                )
                if h:
                    add = add + jnp.where(high_y, pltpu.roll(y, (LANES - half - 64 - half * q) % LANES, 1), 0.0)
                else:
                    add = add + jnp.where(low_y, pltpu.roll(y, (-half * q) % LANES, 1), 0.0)
                for c in range(5):
                    at = c * half + 4 * q
                    rows4 = rx_recv[d, h, at : at + 4, :] + add[4 * c : 4 * c + 4, :]
                    rx_recv[d, h, at : at + 4, :] = rows4
        for c in range(5):
            for h in range(2):
                for f in range(2):
                    at = c * half + f * (half - 1)
                    source = (f * 5 + c) * 2 + h
                    rx_recv[d, h, at : at + 1, :] = (
                        rx_recv[d, h, at : at + 1, :] + x[source : source + 1, :]
                    )
    for c in range(blocks):
        part = pl.ds(c * 5 * half, 5 * half)
        flag = covered[0:1, :][0, c]
        taken = rx_recv[cover_col[0:1, :][0, c]]
        for h in range(2):
            coarse_next[part, tile_at(h)] = jnp.where(flag > 0, taken[h], coarse[part, tile_at(h)])
    store_coarse = pltpu.make_async_copy(coarse_next, coarse_out, out_sem.at[0])
    store_coarse.start()

    for copies in (req_copies, reqx_copies, rep_copies, rx_copies):
        for d in copies:
            copies[d].wait_send()
    for store in stores:
        store.wait()
    store_coarse.wait()


def body(fine_state, coarse_state, neighbours, coarse_sources, covering):
    boxes, comps, edge, plane = fine_state.shape
    blocks, _, half, small = coarse_state.shape
    line = lax.axis_size("gy") * lax.axis_size("gz")
    columns = lax.axis_size("gx")
    faces = boxes * 6
    slots = -(-faces // line)
    dims = (line, columns, lax.axis_size("gz"), boxes, blocks, edge, half, slots)
    fine_rows = boxes * comps * edge
    coarse_rows = blocks * comps * half
    f32, i32 = jnp.float32, jnp.int32
    vmem = pltpu.VMEM
    dma = pltpu.SemaphoreType.DMA
    layer = (comps, SUBS, LANES)
    fine_next, coarse_next = pl.pallas_call(
        functools.partial(kernel, dims),
        out_shape=(
            pltpu.VMEM((fine_rows, plane), f32),
            pltpu.VMEM((coarse_rows, small), f32),
        ),
        in_specs=[pl.BlockSpec(memory_space=pltpu.HBM)] * 5,
        out_specs=(pl.BlockSpec(memory_space=pl.ANY),) * 2,
        scratch_shapes=[
            vmem((fine_rows, plane), f32),
            vmem((coarse_rows, small), f32),
            vmem((plane // LANES, fine_rows, LANES), f32),
            vmem((faces + 6 * blocks,) + layer, f32),
            vmem((2, 2 * coarse_rows, LANES), f32),
            vmem((2, blocks * comps * SUBS, LANES), f32),
            vmem((faces * comps * SUBS, LANES), f32),
            vmem((boxes, 2, comps * half, LANES), f32),
            vmem((coarse_rows, small), f32),
            vmem((boxes, 6), i32),
            vmem((boxes, 6), i32),
            vmem((1, blocks), i32),
            vmem((24, LANES), i32),
            vmem((line, SUBS, LANES), i32),
            vmem((line, SUBS, LANES), i32),
            vmem((columns, SUBS, LANES), i32),
            vmem((columns, SUBS, LANES), i32),
            vmem((line, slots) + layer, f32),
            vmem((line * slots,) + layer, f32),
            vmem((columns, 2, comps * half, LANES), f32),
            vmem((columns, 2, comps * half, LANES), f32),
            vmem((boxes, comps, edge, LANES), f32),
            vmem((boxes, 64, LANES), f32),
            vmem((columns, 64, LANES), f32),
            vmem((columns, 64, LANES), f32),
            dma((5,)),
            dma((1 + plane // LANES,)),
        ]
        + [dma((line,)), dma((line,)), dma((columns,)), dma((columns,))]
        + [dma((line,)), dma((line,)), dma((3 * columns,)), dma((3 * columns,))],
        compiler_params=pltpu.CompilerParams(
            collective_id=0, has_side_effects=True, vmem_limit_bytes=60 * 1024 * 1024
        ),
    )(
        fine_state.reshape(fine_rows, plane),
        coarse_state.reshape(coarse_rows, small),
        neighbours,
        coarse_sources,
        covering.reshape(1, blocks),
    )
    return fine_next.reshape(fine_state.shape), coarse_next.reshape(coarse_state.shape)


def solution(mesh):
    spec = ("gx", "gy", "gz")
    wide = P(spec, None, None, None)
    return jax.shard_map(
        body,
        mesh=mesh,
        in_specs=(wide, wide, P(spec, None), P(spec, None), P(spec)),
        out_specs=(wide, wide),
        check_vma=False,
    )
```

```python
import functools
import jax
import jax.numpy as jnp
from jax import lax
from jax.experimental import pallas as pl
from jax.experimental.pallas import tpu as pltpu
from jax.sharding import PartitionSpec as P

GAMMA = 5.0 / 3.0
COURANT = 0.12
LANES = 128
SUBS = 8
MESH = pl.DeviceIdType.MESH


def primitives(u):
    inverse = 1.0 / u[0]
    speeds = [u[1] * inverse, u[2] * inverse, u[3] * inverse]
    kinetic = 0.5 * (u[1] * speeds[0] + u[2] * speeds[1] + u[3] * speeds[2])
    pressure = (GAMMA - 1.0) * (u[4] - kinetic)
    square = GAMMA * pressure * inverse
    return speeds, pressure, square * lax.rsqrt(square)


def physical(u, prim, normal):
    speeds, pressure, sound = prim
    across = speeds[normal - 1]
    f = [u[normal], u[1] * across, u[2] * across, u[3] * across, (u[4] + pressure) * across]
    f[normal] = f[normal] + pressure
    return f, jnp.abs(across) + sound


def twice_flux(left, right):
    (ul, fl, sl), (ur, fr, sr) = left, right
    fastest = jnp.maximum(sl, sr)
    return [(a + b) - fastest * (d - c) for a, b, c, d in zip(fl, fr, ul, ur)]


def moved(u, f, s, normal, move):
    ud = [move(x) for x in u]
    fd = [ud[normal] if k == 0 else move(f[k]) for k in range(5)]
    return ud, fd, move(s)


def split_dot(x, table, terms):
    total = None
    for term in range(terms):
        part = x.astype(jnp.bfloat16)
        if term < terms - 1:
            x = x - part.astype(jnp.float32)
        add = jnp.dot(part, table, preferred_element_type=jnp.float32)
        total = add if total is None else total + add
    return total


def iota(shape, dim):
    return lax.broadcasted_iota(jnp.int32, shape, dim)


def lane_total(x):
    for shift in (1, 2, 4, 8, 16, 32, 64):
        x = x + pltpu.roll(x, shift, 1)
    return x


def kernel(
    dims,
    fine_hbm, coarse_hbm, neigh_hbm, csrc_hbm, cov_hbm,
    fine_out, coarse_out,
    fine, coarse, nxt_state, table, widened, rows_y, flux_d, restr, coarse_next,
    neigh, csrc, cov, ids, req_send, req_recv, reqx_send, reqx_recv, rep_send, replies, rx_send, rx_recv,
    carried, pooled, pool_send, pool_recv,
    in_sem, out_sem, req_ss, req_rs, reqx_ss, reqx_rs, rep_ss, rep_rs, rx_ss, rx_rs,
):
    line, columns, gz_size, boxes, blocks, edge, half, slots = dims
    f32, i32 = jnp.float32, jnp.int32
    plane = edge * edge
    tiles = plane // LANES
    quarters = edge // SUBS
    faces = boxes * 6
    per_tile = LANES // edge
    gx = lax.axis_index("gx")
    gy = lax.axis_index("gy")
    gz = lax.axis_index("gz")
    me = gy * gz_size + gz

    def line_dev(p):
        return (gx, lax.div(p, gz_size), lax.rem(p, gz_size))

    def col_dev(x):
        return (x, gy, gz)

    def tile_at(t):
        return pl.ds(t * LANES, LANES)

    load_fine = [
        pltpu.make_async_copy(fine_hbm.at[:, tile_at(t)], fine.at[t], in_sem.at[5 + t])
        for t in range(tiles)
    ]
    load_coarse = [
        pltpu.make_async_copy(coarse_hbm.at[:, tile_at(t)], coarse.at[t], in_sem.at[t])
        for t in range(2)
    ]
    load_ids = [
        pltpu.make_async_copy(a, b, in_sem.at[2 + i])
        for i, (a, b) in enumerate(((neigh_hbm, neigh), (csrc_hbm, csrc), (cov_hbm, cov)))
    ]
    for load in load_ids:
        load.start()
    for load in load_fine + load_coarse:
        load.start()

    barrier = pltpu.get_barrier_semaphore()
    for d in range(1, line):
        pl.semaphore_signal(barrier, 1, device_id=line_dev(lax.rem(me + d, line)), device_id_type=MESH)
    for d in range(1, columns):
        pl.semaphore_signal(barrier, 1, device_id=col_dev(lax.rem(gx + d, columns)), device_id_type=MESH)

    for load in load_ids:
        load.wait()
    ids[...] = jnp.full((24, LANES), -1, i32)
    ids[0:boxes, 0:6] = neigh[...]
    ids[8 : 8 + boxes, 0:6] = csrc[...]
    ids[16:17, 0:blocks] = cov[...]
    lane8 = iota((SUBS, LANES), 1)
    sub8 = iota((SUBS, LANES), 0)

    def in_row(tile):
        row = tile[0:1, :]
        for b in range(1, boxes):
            lane1 = lane8[0:1, :]
            row = jnp.where(lane1 >= 6 * b, pltpu.roll(tile, 6 * b, 1)[b : b + 1, :], row)
        return jnp.broadcast_to(row, (line, LANES))

    lane = iota((line, LANES), 1)
    sub = iota((line, LANES), 0)
    near = in_row(ids[0:8, :])
    far = in_row(ids[8:16, :])
    is_fine = near >= 0
    near_dev = lax.div(near, jnp.full_like(near, boxes))
    far_dev = lax.div(far, jnp.full_like(far, blocks))
    side = lane
    for b in range(1, boxes):
        side = jnp.where(lane >= 6 * b, lane - 6 * b, side)
    facing = jnp.bitwise_xor(side, 1)
    code = jnp.where(
        is_fine,
        (near - near_dev * boxes) * 6 + facing,
        faces + (far - far_dev * blocks) * 6 + facing,
    )
    away = jnp.where(is_fine, near_dev, far_dev) - gx * line - me
    away = jnp.where(away < 0, away + line, away)
    match = (away == sub) & (lane < faces)
    ones = jnp.where(match, 1, 0)
    run = ones
    for shift in (1, 2, 4, 8):
        run = run + jnp.where(lane >= shift, pltpu.roll(run, shift, 1), 0)
    rank = run - ones
    asked = jnp.zeros((line, LANES), i32)
    for k in range(slots):
        asked = jnp.where(lane == k, lane_total(jnp.where(match & (rank == k), code, 0)), asked)
    for d in range(line):
        req_send[d] = jnp.broadcast_to(asked[d : d + 1, :], (SUBS, LANES))
    place = jnp.where(match & (rank < slots), sub * slots + rank, 0)
    place_tile = place[0:SUBS, :]
    for part in range(1, line // SUBS):
        place_tile = place_tile + place[part * SUBS : (part + 1) * SUBS, :]
    for shift in (1, 2, 4):
        place_tile = place_tile + pltpu.roll(place_tile, shift, 0)

    cover = jnp.broadcast_to(ids[16:17, :], (SUBS, LANES))
    cover_dev = lax.div(cover, jnp.full_like(cover, boxes))
    cover_col = lax.div(cover_dev, jnp.full_like(cover, line)) - gx
    cover_col = jnp.where(cover_col < 0, cover_col + columns, cover_col)
    covered = cover >= 0
    wanted = lane_total(
        jnp.where(covered & (cover_col == sub8), cover - cover_dev * boxes, 0)
    )
    for d in range(columns):
        reqx_send[d] = jnp.broadcast_to(wanted[d : d + 1, :], (SUBS, LANES))
    cover_col = jnp.where(covered, cover_col, 0)
    covered = jnp.where(covered, 1, 0)

    src = iota((4 * LANES, LANES), 0)
    col = iota((4 * LANES, LANES), 1)
    shrink = jnp.where(
        ((src // (2 * edge)) == col // half) & ((src & (edge - 1)) // 2 == (col & (half - 1))),
        0.125,
        0.0,
    ).astype(jnp.bfloat16)

    tall_lane = iota((edge, LANES), 1)
    tall_row = iota((edge, LANES), 0)
    not_last_x = tall_row < edge - 1
    not_last_z = (tall_lane & (edge - 1)) < edge - 1

    def box_step(half_box, b):
        def load(t):
            return [
                fine[t, pl.ds(pl.multiple_of((b * 5 + c) * edge, edge), edge), :]
                for c in range(5)
            ]

        first = half_box * (tiles // 2)
        cur = load(first)
        prim = primitives(cur)
        if half_box:
            before = [carried[b, c] for c in range(5)]
        else:
            before = [jnp.zeros((edge, LANES), f32)] * 5
        for t in range(first, first + tiles // 2):
            if t < tiles - 1:
                after = load(t + 1)
                after_prim = primitives(after)
            else:
                after, after_prim = cur, prim
            f, s = physical(cur, prim, 1)
            right = moved(cur, f, s, 1, lambda x: pltpu.roll(x, edge - 1, 0))
            flux = [jnp.where(not_last_x, x, 0.0) for x in twice_flux((cur, f, s), right)]
            step = [x - pltpu.roll(x, 1, 0) for x in flux]
            f, s = physical(cur, prim, 3)
            right = moved(cur, f, s, 3, lambda x: pltpu.roll(x, LANES - 1, 1))
            flux = [jnp.where(not_last_z, x, 0.0) for x in twice_flux((cur, f, s), right)]
            step = [a + (x - pltpu.roll(x, 1, 1)) for a, x in zip(step, flux)]
            f, s = physical(cur, prim, 2)
            fa, sa = physical(after, after_prim, 2)

            def up(here, there):
                return pltpu.roll(jnp.where(tall_lane < edge, there, here), LANES - edge, 1)

            ud = [up(x, y) for x, y in zip(cur, after)]
            fd = [ud[2]] + [up(x, y) for x, y in zip(f[1:], fa[1:])]
            flux = twice_flux((cur, f, s), (ud, fd, up(s, sa)))
            if t == tiles - 1:
                flux = [jnp.where(tall_lane < LANES - edge, x, 0.0) for x in flux]
            for c in range(5):
                low = pltpu.roll(
                    jnp.where(tall_lane >= LANES - edge, before[c], flux[c]), edge, 1
                )
                total = step[c] + (flux[c] - low)
                nxt_state[t, pl.ds(pl.multiple_of((b * 5 + c) * edge, edge), edge), :] = (
                    cur[c] - (0.5 * COURANT) * total
                )
            before = flux
            cur, prim = after, after_prim
        if not half_box:
            for c in range(5):
                carried[b, c] = before[c]

    pairs = 5 * half
    rx_copies = {}

    def step_half(h):
        def one_box(b, carry):
            box_step(h, b)
            start = b * 5 * edge
            parts = [
                nxt_state[t, pl.ds(start, pairs, stride=2), :]
                + nxt_state[t, pl.ds(start + 1, pairs, stride=2), :]
                for t in range(4 * h, 4 * h + 4)
            ]
            restr[b, h] = split_dot(jnp.concatenate(parts, axis=1), shrink, 2)
            return carry

        lax.fori_loop(0, boxes, one_box, 0)

    def send_half(h):
        for d in range(columns):
            if d and not h:
                reqx_copies[d].wait_recv()
            if d:
                rx_send[d, h] = restr[reqx_recv[d][0:1, :][0, 0], h]
                rx_copies[d, h] = pltpu.make_async_remote_copy(
                    rx_send.at[d, h], rx_recv.at[d, h], rx_ss.at[d * 3 + h], rx_rs.at[d * 3 + h],
                    device_id=col_dev(lax.rem(gx + columns - d, columns)), device_id_type=MESH,
                )
                rx_copies[d, h].start()
            else:
                rx_recv[d, h] = restr[wanted[0:1, :][0, 0], h]

    for load in load_fine:
        load.wait()
    step_half(0)

    in_edge = lane8 & (edge - 1)
    group = lane8 // edge
    pl.semaphore_wait(barrier, line - 1 + columns - 1)

    req_copies = {}
    for d in range(1, line):
        req_copies[d] = pltpu.make_async_remote_copy(
            req_send.at[d], req_recv.at[d], req_ss.at[d], req_rs.at[d],
            device_id=line_dev(lax.rem(me + d, line)), device_id_type=MESH,
        )
        req_copies[d].start()
    reqx_copies = {}
    for d in range(1, columns):
        reqx_copies[d] = pltpu.make_async_remote_copy(
            reqx_send.at[d], reqx_recv.at[d], reqx_ss.at[d], reqx_rs.at[d],
            device_id=col_dev(lax.rem(gx + d, columns)), device_id_type=MESH,
        )
        reqx_copies[d].start()


    def fine_layers(bc, carry):
        b = lax.div(bc, 5)
        c = bc - b * 5
        row = pl.multiple_of(bc * edge, edge)
        z_low = jnp.zeros((SUBS, LANES), f32)
        z_high = jnp.zeros((SUBS, LANES), f32)
        y_low = jnp.zeros((SUBS, LANES), f32)
        y_high = jnp.zeros((SUBS, LANES), f32)
        for q in range(quarters):
            for t in range(tiles):
                block = fine[t, pl.ds(row + q * SUBS, SUBS), :]
                s = q * SUBS + t
                z_low = jnp.where(in_edge == s, pltpu.roll(block, s, 1), z_low)
                z_high = jnp.where(in_edge == s, pltpu.roll(block, (s - edge + 1) % LANES, 1), z_high)
                if t == 0:
                    y_low = jnp.where(group == q, pltpu.roll(block, q * edge, 1), y_low)
                if t == tiles - 1:
                    y_high = jnp.where(
                        group == q, pltpu.roll(block, (q * edge - (LANES - edge)) % LANES, 1), y_high
                    )
        at = pl.ds(pl.multiple_of(c * SUBS, SUBS), SUBS)
        for side, layer in enumerate((y_low, y_high, z_low, z_high)):
            table[b * 6 + 2 + side, at, :] = layer
        return carry

    lax.fori_loop(0, boxes * 5, fine_layers, 0, unroll=2)
    for b in range(boxes):
        for f in range(2):
            for t in range(tiles):
                table[b * 6 + f, pl.ds(t, 5, stride=SUBS), :] = fine[
                    t, pl.ds(b * 5 * edge + f * (edge - 1), 5, stride=edge), :
                ]

    send_half(0)

    for load in load_coarse:
        load.wait()
    small = half * half
    src = iota((small, 2 * LANES), 0)
    col = iota((small, 2 * LANES), 1)
    lane_w = col & (LANES - 1)
    y_src = (lane_w // edge) * ((half - 1) * half) + (lane_w & (edge - 1)) // 2
    z_j = 4 * (lane_w & (SUBS - 1)) + lane_w // edge
    z_src = (z_j // 2) * half + ((lane_w & (edge - 1)) // SUBS) * (half - 1)
    y_ok = (col < LANES) & (lane_w < 2 * edge) & (src == y_src)
    z_ok = (col >= LANES) & ((lane_w & (edge - 1)) < 2 * SUBS) & (src == z_src)
    lateral_table = jnp.where(y_ok | z_ok, 1.0, 0.0).astype(jnp.bfloat16)
    lateral = split_dot(jnp.concatenate([coarse[0], coarse[1]], axis=1), lateral_table, 3)
    rows = blocks * 5 * half
    for part in range(2):
        piece = lateral[:, part * LANES : (part + 1) * LANES]
        widened[part, pl.ds(0, rows, stride=2), :] = piece
        widened[part, pl.ds(1, rows, stride=2), :] = piece
    z_group = in_edge // SUBS

    def coarse_layers(bc, carry):
        b = lax.div(bc, 5)
        c = bc - b * 5
        row = pl.multiple_of(bc * edge, edge)
        for f in range(2):
            y = jnp.zeros((SUBS, LANES), f32)
            z = jnp.zeros((SUBS, LANES), f32)
            for q in range(quarters):
                block = widened[0, pl.ds(row + q * SUBS, SUBS), :]
                y = jnp.where(group == q, pltpu.roll(block, (edge * (q - f)) % LANES, 1), y)
                block = widened[1, pl.ds(row + q * SUBS, SUBS), :]
                z = jnp.where(z_group == q, pltpu.roll(block, (SUBS * (q - f)) % LANES, 1), z)
            at = pl.ds(pl.multiple_of(c * SUBS, SUBS), SUBS)
            table[faces + b * 6 + 2 + f, at, :] = y
            table[faces + b * 6 + 4 + f, at, :] = z
        return carry

    lax.fori_loop(0, blocks * 5, coarse_layers, 0, unroll=4)

    src = iota((LANES, LANES), 0)
    col = iota((LANES, LANES), 1)
    x_table = jnp.where(
        src == (col // (2 * edge)) * half + (col & (edge - 1)) // 2, 1.0, 0.0
    ).astype(jnp.bfloat16)
    for f in range(2):
        for t in range(SUBS):
            ends = coarse[t // 4, pl.ds(f * (half - 1), blocks * 5, stride=half), :]
            rows_y[f, pl.ds(t, blocks * 5, stride=SUBS), :] = pltpu.roll(
                ends, (-2 * half * (t % 4)) % LANES, 1
            )
        spread = split_dot(rows_y[f], x_table, 3)
        for b in range(blocks):
            at = b * 5 * SUBS
            table[faces + b * 6 + f] = spread[at : at + 5 * SUBS, :]

    my_codes = asked[0:1, :]
    rep_copies = {}
    for d in list(range(1, line)) + [0]:
        if d:
            req_copies[d].wait_recv()
            codes = req_recv[d][0:1, :]
        else:
            codes = my_codes
        for k in range(slots):
            layer = table[codes[0, k]]
            if d:
                rep_send[d, k] = layer
            else:
                replies[d * slots + k] = layer
        if d:
            rep_copies[d] = pltpu.make_async_remote_copy(
                rep_send.at[d], replies.at[pl.ds(d * slots, slots)], rep_ss.at[d], rep_rs.at[d],
                device_id=line_dev(lax.rem(me + line - d, line)), device_id_type=MESH,
            )
            rep_copies[d].start()

    step_half(1)
    send_half(1)

    src = iota((2 * LANES, LANES), 0)
    col = iota((2 * LANES, LANES), 1)
    upper = src // LANES
    src = src & (LANES - 1)
    src_t = src & (SUBS - 1)
    src_q = (src & (edge - 1)) // SUBS
    to_z = ((src_t & 3) * 2 + src // (2 * edge)) * half + upper * SUBS + (src_t // 4) * 4 + src_q
    to_y = upper * (LANES // 2) + src // 2
    pool_z = jnp.where(col == to_z, 0.125, 0.0).astype(jnp.bfloat16)
    pool_y = jnp.where(col == to_y, 0.125, 0.0).astype(jnp.bfloat16)

    for d in range(1, line):
        rep_copies[d].wait_recv()
    for b in range(boxes):
        for g in range(6):
            ghost_all = replies[place_tile[0:1, :][0, b * 6 + g]]
            own_all = table[b * 6 + g]
            normal = g // 2 + 1
            pair = []
            for layers in (ghost_all, own_all):
                u = [layers[c * SUBS : (c + 1) * SUBS, :] for c in range(5)]
                pair.append((u,) + physical(u, primitives(u), normal))
            if g % 2:
                flux = twice_flux(pair[1], pair[0])
                scale = -0.5 * COURANT
            else:
                flux = twice_flux(pair[0], pair[1])
                scale = 0.5 * COURANT
            for c in range(5):
                flux_d[pl.ds(((b * 6 + g) * 5 + c) * SUBS, SUBS), :] = scale * flux[c]

    for b in range(boxes):
        at = b * 6 * 5 * SUBS
        parts = [flux_d[pl.ds(at + e, 20, stride=4), :] for e in range(4)]
        pooled[b, 0:20, :] = split_dot(jnp.concatenate(parts, axis=1), shrink, 2)
        for g, pool in ((2, pool_y), (4, pool_z)):
            parts = []
            for f in (g, g + 1):
                at = (b * 6 + f) * 5 * SUBS
                parts.append(flux_d[pl.ds(at, 20, stride=2), :] + flux_d[pl.ds(at + 1, 20, stride=2), :])
            pooled[b, 10 * g : 10 * g + 20, :] = split_dot(jnp.concatenate(parts, axis=1), pool, 2)
        pooled[b, 60:64, :] = jnp.zeros((4, LANES), f32)
    for d in range(columns):
        if d:
            pool_send[d] = pooled[reqx_recv[d][0:1, :][0, 0]]
            rx_copies[d, 2] = pltpu.make_async_remote_copy(
                pool_send.at[d], pool_recv.at[d], rx_ss.at[d * 3 + 2], rx_rs.at[d * 3 + 2],
                device_id=col_dev(lax.rem(gx + columns - d, columns)), device_id_type=MESH,
            )
            rx_copies[d, 2].start()
        else:
            pool_recv[d] = pooled[wanted[0:1, :][0, 0]]

    def add_faces(bc, carry):
        b = lax.div(bc, 5)
        c = bc - b * 5
        row = pl.multiple_of(bc * edge, edge)
        d = [
            flux_d[pl.ds(pl.multiple_of(((b * 6 + g) * 5 + c) * SUBS, SUBS), SUBS), :]
            for g in range(6)
        ]
        for q in range(quarters):
            for t in range(tiles):
                s = q * SUBS + t
                at = (t, pl.ds(row + q * SUBS, SUBS), slice(None))
                block = nxt_state[at]
                block = block + jnp.where(
                    in_edge == 0,
                    pltpu.roll(d[4], (-s) % LANES, 1),
                    jnp.where(in_edge == edge - 1, pltpu.roll(d[5], (edge - 1 - s) % LANES, 1), 0.0),
                )
                if t == 0:
                    block = block + jnp.where(group == 0, pltpu.roll(d[2], (-q * edge) % LANES, 1), 0.0)
                if t == tiles - 1:
                    block = block + jnp.where(
                        group == per_tile - 1,
                        pltpu.roll(d[3], (LANES - edge - q * edge) % LANES, 1),
                        0.0,
                    )
                if q == 0:
                    block = block + jnp.where(sub8 == 0, d[0][t : t + 1, :], 0.0)
                if q == quarters - 1:
                    block = block + jnp.where(sub8 == SUBS - 1, d[1][t : t + 1, :], 0.0)
                nxt_state[at] = block
        return carry

    lax.fori_loop(0, boxes * 5, add_faces, 0)

    stores = []
    for t in range(tiles):
        stores.append(
            pltpu.make_async_copy(nxt_state.at[t], fine_out.at[:, tile_at(t)], out_sem.at[1 + t])
        )
        stores[-1].start()

    wide20 = iota((20, LANES), 1)
    low_z = (wide20 & (half - 1)) == 0
    high_z = (wide20 & (half - 1)) == half - 1
    low_y = wide20 < half
    high_y = wide20 >= LANES - half
    for d in range(columns):
        if d:
            for h in range(3):
                rx_copies[d, h].wait_recv()
        x, y, z = (pool_recv[d, pl.ds(20 * i, 20), :] for i in range(3))
        for q in range(quarters):
            for h in range(2):
                s = h * 4 + q
                add = jnp.where(
                    low_z,
                    pltpu.roll(z, (-s) % LANES, 1),
                    jnp.where(high_z, pltpu.roll(z, (half - 1 - SUBS - s) % LANES, 1), 0.0),
                )
                if h:
                    add = add + jnp.where(high_y, pltpu.roll(y, (LANES - half - 64 - half * q) % LANES, 1), 0.0)
                else:
                    add = add + jnp.where(low_y, pltpu.roll(y, (-half * q) % LANES, 1), 0.0)
                for c in range(5):
                    at = c * half + 4 * q
                    rows4 = rx_recv[d, h, at : at + 4, :] + add[4 * c : 4 * c + 4, :]
                    rx_recv[d, h, at : at + 4, :] = rows4
        for c in range(5):
            for h in range(2):
                for f in range(2):
                    at = c * half + f * (half - 1)
                    source = (f * 5 + c) * 2 + h
                    rx_recv[d, h, at : at + 1, :] = (
                        rx_recv[d, h, at : at + 1, :] + x[source : source + 1, :]
                    )
    for c in range(blocks):
        part = pl.ds(c * 5 * half, 5 * half)
        flag = covered[0:1, :][0, c]
        taken = rx_recv[cover_col[0:1, :][0, c]]
        for h in range(2):
            coarse_next[part, tile_at(h)] = jnp.where(flag > 0, taken[h], coarse[h, part, :])
    store_coarse = pltpu.make_async_copy(coarse_next, coarse_out, out_sem.at[0])
    store_coarse.start()

    for copies in (req_copies, reqx_copies, rep_copies, rx_copies):
        for d in copies:
            copies[d].wait_send()
    for store in stores:
        store.wait()
    store_coarse.wait()


def write_kernel(fine, coarse, fine_out, coarse_out, sem):
    rows = fine.shape[0] // 4
    copies = [
        pltpu.make_async_copy(
            fine.at[pl.ds(i * rows, rows), :], fine_out.at[pl.ds(i * rows, rows), :], sem.at[i]
        )
        for i in range(4)
    ]
    copies.append(pltpu.make_async_copy(coarse, coarse_out, sem.at[4]))
    for copy in copies:
        copy.start()
    for copy in copies:
        copy.wait()


def body(fine_state, coarse_state, neighbours, coarse_sources, covering):
    boxes, comps, edge, plane = fine_state.shape
    blocks, _, half, small = coarse_state.shape
    line = lax.axis_size("gy") * lax.axis_size("gz")
    columns = lax.axis_size("gx")
    faces = boxes * 6
    slots = -(-faces // line)
    dims = (line, columns, lax.axis_size("gz"), boxes, blocks, edge, half, slots)
    fine_rows = boxes * comps * edge
    coarse_rows = blocks * comps * half
    f32, i32 = jnp.float32, jnp.int32
    vmem = pltpu.VMEM
    dma = pltpu.SemaphoreType.DMA
    layer = (comps * SUBS, LANES)
    fine_next, coarse_next = pl.pallas_call(
        functools.partial(kernel, dims),
        out_shape=(
            pltpu.VMEM((fine_rows, plane), f32),
            pltpu.VMEM((coarse_rows, small), f32),
        ),
        in_specs=[pl.BlockSpec(memory_space=pltpu.HBM)] * 5,
        out_specs=(pl.BlockSpec(memory_space=pl.ANY),) * 2,
        scratch_shapes=[
            vmem((plane // LANES, fine_rows, LANES), f32),
            vmem((2, coarse_rows, LANES), f32),
            vmem((plane // LANES, fine_rows, LANES), f32),
            vmem((faces + 6 * blocks,) + layer, f32),
            vmem((2, 2 * coarse_rows, LANES), f32),
            vmem((2, blocks * comps * SUBS, LANES), f32),
            vmem((faces * comps * SUBS, LANES), f32),
            vmem((boxes, 2, comps * half, LANES), f32),
            vmem((coarse_rows, small), f32),
            vmem((boxes, 6), i32),
            vmem((boxes, 6), i32),
            vmem((1, blocks), i32),
            vmem((24, LANES), i32),
            vmem((line, SUBS, LANES), i32),
            vmem((line, SUBS, LANES), i32),
            vmem((columns, SUBS, LANES), i32),
            vmem((columns, SUBS, LANES), i32),
            vmem((line, slots) + layer, f32),
            vmem((line * slots,) + layer, f32),
            vmem((columns, 2, comps * half, LANES), f32),
            vmem((columns, 2, comps * half, LANES), f32),
            vmem((boxes, comps, edge, LANES), f32),
            vmem((boxes, 64, LANES), f32),
            vmem((columns, 64, LANES), f32),
            vmem((columns, 64, LANES), f32),
            dma((5 + plane // LANES,)),
            dma((1 + plane // LANES,)),
        ]
        + [dma((line,)), dma((line,)), dma((columns,)), dma((columns,))]
        + [dma((line,)), dma((line,)), dma((3 * columns,)), dma((3 * columns,))],
        compiler_params=pltpu.CompilerParams(
            collective_id=0, has_side_effects=True, vmem_limit_bytes=60 * 1024 * 1024
        ),
    )(
        fine_state.reshape(fine_rows, plane),
        coarse_state.reshape(coarse_rows, small),
        neighbours,
        coarse_sources,
        covering.reshape(1, blocks),
    )
    fine_next, coarse_next = pl.pallas_call(
        write_kernel,
        out_shape=(
            pltpu.HBM((fine_rows, plane), f32),
            pltpu.HBM((coarse_rows, small), f32),
        ),
        in_specs=[pl.BlockSpec(memory_space=pl.ANY)] * 2,
        out_specs=(pl.BlockSpec(memory_space=pl.ANY),) * 2,
        scratch_shapes=[dma((5,))],
    )(fine_next, coarse_next)
    return fine_next.reshape(fine_state.shape), coarse_next.reshape(coarse_state.shape)


def solution(mesh):
    spec = ("gx", "gy", "gz")
    wide = P(spec, None, None, None)
    return jax.shard_map(
        body,
        mesh=mesh,
        in_specs=(wide, wide, P(spec, None), P(spec, None), P(spec)),
        out_specs=(wide, wide),
        check_vma=False,
    )
```

```python
import functools
import jax
import jax.numpy as jnp
from jax import lax
from jax.experimental import pallas as pl
from jax.experimental.pallas import tpu as pltpu
from jax.sharding import PartitionSpec as P

GAMMA = 5.0 / 3.0
COURANT = 0.12
LANES = 128
SUBS = 8
MESH = pl.DeviceIdType.MESH


def primitives(u):
    inverse = 1.0 / u[0]
    speeds = [u[1] * inverse, u[2] * inverse, u[3] * inverse]
    kinetic = 0.5 * (u[1] * speeds[0] + u[2] * speeds[1] + u[3] * speeds[2])
    pressure = (GAMMA - 1.0) * (u[4] - kinetic)
    square = GAMMA * pressure * inverse
    return speeds, pressure, square * lax.rsqrt(square)


def physical(u, prim, normal):
    speeds, pressure, sound = prim
    across = speeds[normal - 1]
    f = [u[normal], u[1] * across, u[2] * across, u[3] * across, (u[4] + pressure) * across]
    f[normal] = f[normal] + pressure
    return f, jnp.abs(across) + sound


def twice_flux(left, right):
    (ul, fl, sl), (ur, fr, sr) = left, right
    fastest = jnp.maximum(sl, sr)
    return [(a + b) - fastest * (d - c) for a, b, c, d in zip(fl, fr, ul, ur)]


def moved(u, f, s, normal, move):
    ud = [move(x) for x in u]
    fd = [ud[normal] if k == 0 else move(f[k]) for k in range(5)]
    return ud, fd, move(s)


def split_dot(x, table, terms):
    total = None
    for term in range(terms):
        part = x.astype(jnp.bfloat16)
        if term < terms - 1:
            x = x - part.astype(jnp.float32)
        add = jnp.dot(part, table, preferred_element_type=jnp.float32)
        total = add if total is None else total + add
    return total


def iota(shape, dim):
    return lax.broadcasted_iota(jnp.int32, shape, dim)


def lane_total(x):
    for shift in (1, 2, 4, 8, 16, 32, 64):
        x = x + pltpu.roll(x, shift, 1)
    return x


def kernel(
    dims,
    fine_hbm, coarse_hbm, neigh_hbm, csrc_hbm, cov_hbm,
    fine_out, coarse_out,
    fine, coarse, nxt_state, table, widened, rows_y, flux_d, restr, coarse_next,
    neigh, csrc, cov, ids, req_send, req_recv, reqx_send, reqx_recv, rep_send, replies, rx_send, rx_recv,
    carried, pooled, pool_send, pool_recv,
    in_sem, out_sem, req_ss, req_rs, reqx_ss, reqx_rs, rep_ss, rep_rs, rx_ss, rx_rs,
):
    line, columns, gz_size, boxes, blocks, edge, half, slots = dims
    f32, i32 = jnp.float32, jnp.int32
    plane = edge * edge
    tiles = plane // LANES
    quarters = edge // SUBS
    faces = boxes * 6
    per_tile = LANES // edge
    gx = lax.axis_index("gx")
    gy = lax.axis_index("gy")
    gz = lax.axis_index("gz")
    me = gy * gz_size + gz

    def line_dev(p):
        return (gx, lax.div(p, gz_size), lax.rem(p, gz_size))

    def col_dev(x):
        return (x, gy, gz)

    def tile_at(t):
        return pl.ds(t * LANES, LANES)

    load_fine = [
        pltpu.make_async_copy(fine_hbm.at[:, tile_at(t)], fine.at[t], in_sem.at[5 + t])
        for t in range(tiles)
    ]
    load_coarse = [
        pltpu.make_async_copy(coarse_hbm.at[:, tile_at(t)], coarse.at[t], in_sem.at[t])
        for t in range(2)
    ]
    load_ids = [
        pltpu.make_async_copy(a, b, in_sem.at[2 + i])
        for i, (a, b) in enumerate(((neigh_hbm, neigh), (csrc_hbm, csrc), (cov_hbm, cov)))
    ]
    for load in load_ids:
        load.start()
    for load in load_fine + load_coarse:
        load.start()

    barrier = pltpu.get_barrier_semaphore()
    for d in range(1, line):
        pl.semaphore_signal(barrier, 1, device_id=line_dev(lax.rem(me + d, line)), device_id_type=MESH)
    for d in range(1, columns):
        pl.semaphore_signal(barrier, 1, device_id=col_dev(lax.rem(gx + d, columns)), device_id_type=MESH)

    for load in load_ids:
        load.wait()
    ids[...] = jnp.full((24, LANES), -1, i32)
    ids[0:boxes, 0:6] = neigh[...]
    ids[8 : 8 + boxes, 0:6] = csrc[...]
    ids[16:17, 0:blocks] = cov[...]
    lane8 = iota((SUBS, LANES), 1)
    sub8 = iota((SUBS, LANES), 0)

    def in_row(tile):
        row = tile[0:1, :]
        for b in range(1, boxes):
            lane1 = lane8[0:1, :]
            row = jnp.where(lane1 >= 6 * b, pltpu.roll(tile, 6 * b, 1)[b : b + 1, :], row)
        return jnp.broadcast_to(row, (line, LANES))

    lane = iota((line, LANES), 1)
    sub = iota((line, LANES), 0)
    near = in_row(ids[0:8, :])
    far = in_row(ids[8:16, :])
    is_fine = near >= 0
    near_dev = lax.div(near, jnp.full_like(near, boxes))
    far_dev = lax.div(far, jnp.full_like(far, blocks))
    side = lane
    for b in range(1, boxes):
        side = jnp.where(lane >= 6 * b, lane - 6 * b, side)
    facing = jnp.bitwise_xor(side, 1)
    code = jnp.where(
        is_fine,
        (near - near_dev * boxes) * 6 + facing,
        faces + (far - far_dev * blocks) * 6 + facing,
    )
    away = jnp.where(is_fine, near_dev, far_dev) - gx * line - me
    away = jnp.where(away < 0, away + line, away)
    match = (away == sub) & (lane < faces)
    ones = jnp.where(match, 1, 0)
    run = ones
    for shift in (1, 2, 4, 8):
        run = run + jnp.where(lane >= shift, pltpu.roll(run, shift, 1), 0)
    rank = run - ones
    asked = jnp.zeros((line, LANES), i32)
    for k in range(slots):
        asked = jnp.where(lane == k, lane_total(jnp.where(match & (rank == k), code, 0)), asked)
    for d in range(line):
        req_send[d] = jnp.broadcast_to(asked[d : d + 1, :], (SUBS, LANES))
    place = jnp.where(match & (rank < slots), sub * slots + rank, 0)
    place_tile = place[0:SUBS, :]
    for part in range(1, line // SUBS):
        place_tile = place_tile + place[part * SUBS : (part + 1) * SUBS, :]
    for shift in (1, 2, 4):
        place_tile = place_tile + pltpu.roll(place_tile, shift, 0)

    place_row = place_tile[0:1, :]
    ghost_at = [place_row[0, i] for i in range(faces)]
    own_codes = [asked[0:1, :][0, k] for k in range(slots)]

    cover = jnp.broadcast_to(ids[16:17, :], (SUBS, LANES))
    cover_dev = lax.div(cover, jnp.full_like(cover, boxes))
    cover_col = lax.div(cover_dev, jnp.full_like(cover, line)) - gx
    cover_col = jnp.where(cover_col < 0, cover_col + columns, cover_col)
    covered = cover >= 0
    wanted = lane_total(
        jnp.where(covered & (cover_col == sub8), cover - cover_dev * boxes, 0)
    )
    for d in range(columns):
        reqx_send[d] = jnp.broadcast_to(wanted[d : d + 1, :], (SUBS, LANES))
    cover_col = jnp.where(covered, cover_col, 0)
    covered = jnp.where(covered, 1, 0)
    cover_at = [cover_col[0:1, :][0, c] for c in range(blocks)]
    cover_flag = [covered[0:1, :][0, c] for c in range(blocks)]
    sent_box = [wanted[0:1, :][0, 0]]

    src = iota((4 * LANES, LANES), 0)
    col = iota((4 * LANES, LANES), 1)
    shrink = jnp.where(
        ((src // (2 * edge)) == col // half) & ((src & (edge - 1)) // 2 == (col & (half - 1))),
        0.125,
        0.0,
    ).astype(jnp.bfloat16)

    tall_lane = iota((edge, LANES), 1)
    tall_row = iota((edge, LANES), 0)
    not_last_x = tall_row < edge - 1
    not_last_z = (tall_lane & (edge - 1)) < edge - 1

    def box_step(half_box, b):
        def load(t):
            return [
                fine[t, pl.ds(pl.multiple_of((b * 5 + c) * edge, edge), edge), :]
                for c in range(5)
            ]

        first = half_box * (tiles // 2)
        cur = load(first)
        prim = primitives(cur)
        if half_box:
            before = [carried[b, c] for c in range(5)]
        else:
            before = [jnp.zeros((edge, LANES), f32)] * 5
        for t in range(first, first + tiles // 2):
            if t < tiles - 1:
                after = load(t + 1)
                after_prim = primitives(after)
            else:
                after, after_prim = cur, prim
            f, s = physical(cur, prim, 1)
            right = moved(cur, f, s, 1, lambda x: pltpu.roll(x, edge - 1, 0))
            flux = [jnp.where(not_last_x, x, 0.0) for x in twice_flux((cur, f, s), right)]
            step = [x - pltpu.roll(x, 1, 0) for x in flux]
            f, s = physical(cur, prim, 3)
            right = moved(cur, f, s, 3, lambda x: pltpu.roll(x, LANES - 1, 1))
            flux = [jnp.where(not_last_z, x, 0.0) for x in twice_flux((cur, f, s), right)]
            step = [a + (x - pltpu.roll(x, 1, 1)) for a, x in zip(step, flux)]
            f, s = physical(cur, prim, 2)
            fa, sa = physical(after, after_prim, 2)

            def up(here, there):
                return pltpu.roll(jnp.where(tall_lane < edge, there, here), LANES - edge, 1)

            ud = [up(x, y) for x, y in zip(cur, after)]
            fd = [ud[2]] + [up(x, y) for x, y in zip(f[1:], fa[1:])]
            flux = twice_flux((cur, f, s), (ud, fd, up(s, sa)))
            if t == tiles - 1:
                flux = [jnp.where(tall_lane < LANES - edge, x, 0.0) for x in flux]
            for c in range(5):
                low = pltpu.roll(
                    jnp.where(tall_lane >= LANES - edge, before[c], flux[c]), edge, 1
                )
                total = step[c] + (flux[c] - low)
                nxt_state[t, pl.ds(pl.multiple_of((b * 5 + c) * edge, edge), edge), :] = (
                    cur[c] - (0.5 * COURANT) * total
                )
            before = flux
            cur, prim = after, after_prim
        if not half_box:
            for c in range(5):
                carried[b, c] = before[c]

    pairs = 5 * half
    rx_copies = {}

    def step_half(h):
        def one_box(b, carry):
            box_step(h, b)
            start = b * 5 * edge
            parts = [
                nxt_state[t, pl.ds(start, pairs, stride=2), :]
                + nxt_state[t, pl.ds(start + 1, pairs, stride=2), :]
                for t in range(4 * h, 4 * h + 4)
            ]
            restr[b, h] = split_dot(jnp.concatenate(parts, axis=1), shrink, 2)
            return carry

        lax.fori_loop(0, boxes, one_box, 0)

    def send_half(h):
        for d in range(columns):
            if d:
                rx_send[d, h] = restr[sent_box[d], h]
                rx_copies[d, h] = pltpu.make_async_remote_copy(
                    rx_send.at[d, h], rx_recv.at[d, h], rx_ss.at[d * 3 + h], rx_rs.at[d * 3 + h],
                    device_id=col_dev(lax.rem(gx + columns - d, columns)), device_id_type=MESH,
                )
                rx_copies[d, h].start()
            else:
                rx_recv[d, h] = restr[sent_box[0], h]

    for load in load_fine:
        load.wait()
    step_half(0)

    in_edge = lane8 & (edge - 1)
    group = lane8 // edge
    pl.semaphore_wait(barrier, line - 1 + columns - 1)

    req_copies = {}
    for d in range(1, line):
        req_copies[d] = pltpu.make_async_remote_copy(
            req_send.at[d], req_recv.at[d], req_ss.at[d], req_rs.at[d],
            device_id=line_dev(lax.rem(me + d, line)), device_id_type=MESH,
        )
        req_copies[d].start()
    reqx_copies = {}
    for d in range(1, columns):
        reqx_copies[d] = pltpu.make_async_remote_copy(
            reqx_send.at[d], reqx_recv.at[d], reqx_ss.at[d], reqx_rs.at[d],
            device_id=col_dev(lax.rem(gx + d, columns)), device_id_type=MESH,
        )
        reqx_copies[d].start()


    def fine_layers(bc, carry):
        b = lax.div(bc, 5)
        c = bc - b * 5
        row = pl.multiple_of(bc * edge, edge)
        z_low = jnp.zeros((SUBS, LANES), f32)
        z_high = jnp.zeros((SUBS, LANES), f32)
        y_low = jnp.zeros((SUBS, LANES), f32)
        y_high = jnp.zeros((SUBS, LANES), f32)
        for q in range(quarters):
            for t in range(tiles):
                block = fine[t, pl.ds(row + q * SUBS, SUBS), :]
                s = q * SUBS + t
                z_low = jnp.where(in_edge == s, pltpu.roll(block, s, 1), z_low)
                z_high = jnp.where(in_edge == s, pltpu.roll(block, (s - edge + 1) % LANES, 1), z_high)
                if t == 0:
                    y_low = jnp.where(group == q, pltpu.roll(block, q * edge, 1), y_low)
                if t == tiles - 1:
                    y_high = jnp.where(
                        group == q, pltpu.roll(block, (q * edge - (LANES - edge)) % LANES, 1), y_high
                    )
        at = pl.ds(pl.multiple_of(c * SUBS, SUBS), SUBS)
        for side, layer in enumerate((y_low, y_high, z_low, z_high)):
            table[b * 6 + 2 + side, at, :] = layer
        return carry

    lax.fori_loop(0, boxes * 5, fine_layers, 0, unroll=2)
    for b in range(boxes):
        for f in range(2):
            for t in range(tiles):
                table[b * 6 + f, pl.ds(t, 5, stride=SUBS), :] = fine[
                    t, pl.ds(b * 5 * edge + f * (edge - 1), 5, stride=edge), :
                ]

    for d in range(1, columns):
        reqx_copies[d].wait_recv()
    sent_box += [reqx_recv[d][0:1, :][0, 0] for d in range(1, columns)]
    send_half(0)

    for load in load_coarse:
        load.wait()
    small = half * half
    src = iota((small, 2 * LANES), 0)
    col = iota((small, 2 * LANES), 1)
    lane_w = col & (LANES - 1)
    y_src = (lane_w // edge) * ((half - 1) * half) + (lane_w & (edge - 1)) // 2
    z_j = 4 * (lane_w & (SUBS - 1)) + lane_w // edge
    z_src = (z_j // 2) * half + ((lane_w & (edge - 1)) // SUBS) * (half - 1)
    y_ok = (col < LANES) & (lane_w < 2 * edge) & (src == y_src)
    z_ok = (col >= LANES) & ((lane_w & (edge - 1)) < 2 * SUBS) & (src == z_src)
    lateral_table = jnp.where(y_ok | z_ok, 1.0, 0.0).astype(jnp.bfloat16)
    lateral = split_dot(jnp.concatenate([coarse[0], coarse[1]], axis=1), lateral_table, 3)
    rows = blocks * 5 * half
    for part in range(2):
        piece = lateral[:, part * LANES : (part + 1) * LANES]
        widened[part, pl.ds(0, rows, stride=2), :] = piece
        widened[part, pl.ds(1, rows, stride=2), :] = piece
    z_group = in_edge // SUBS

    def coarse_layers(bc, carry):
        b = lax.div(bc, 5)
        c = bc - b * 5
        row = pl.multiple_of(bc * edge, edge)
        for f in range(2):
            y = jnp.zeros((SUBS, LANES), f32)
            z = jnp.zeros((SUBS, LANES), f32)
            for q in range(quarters):
                block = widened[0, pl.ds(row + q * SUBS, SUBS), :]
                y = jnp.where(group == q, pltpu.roll(block, (edge * (q - f)) % LANES, 1), y)
                block = widened[1, pl.ds(row + q * SUBS, SUBS), :]
                z = jnp.where(z_group == q, pltpu.roll(block, (SUBS * (q - f)) % LANES, 1), z)
            at = pl.ds(pl.multiple_of(c * SUBS, SUBS), SUBS)
            table[faces + b * 6 + 2 + f, at, :] = y
            table[faces + b * 6 + 4 + f, at, :] = z
        return carry

    lax.fori_loop(0, blocks * 5, coarse_layers, 0, unroll=4)

    src = iota((LANES, LANES), 0)
    col = iota((LANES, LANES), 1)
    x_table = jnp.where(
        src == (col // (2 * edge)) * half + (col & (edge - 1)) // 2, 1.0, 0.0
    ).astype(jnp.bfloat16)
    for f in range(2):
        for t in range(SUBS):
            ends = coarse[t // 4, pl.ds(f * (half - 1), blocks * 5, stride=half), :]
            rows_y[f, pl.ds(t, blocks * 5, stride=SUBS), :] = pltpu.roll(
                ends, (-2 * half * (t % 4)) % LANES, 1
            )
        spread = split_dot(rows_y[f], x_table, 3)
        for b in range(blocks):
            at = b * 5 * SUBS
            table[faces + b * 6 + f] = spread[at : at + 5 * SUBS, :]

    rep_copies = {}
    for d in range(1, line):
        req_copies[d].wait_recv()
    codes = [own_codes] + [
        [req_recv[d][0:1, :][0, k] for k in range(slots)] for d in range(1, line)
    ]
    for d in list(range(1, line)) + [0]:
        for k in range(slots):
            layer = table[codes[d][k]]
            if d:
                rep_send[d, k] = layer
            else:
                replies[d * slots + k] = layer
        if d:
            rep_copies[d] = pltpu.make_async_remote_copy(
                rep_send.at[d], replies.at[pl.ds(d * slots, slots)], rep_ss.at[d], rep_rs.at[d],
                device_id=line_dev(lax.rem(me + line - d, line)), device_id_type=MESH,
            )
            rep_copies[d].start()

    step_half(1)
    send_half(1)

    src = iota((2 * LANES, LANES), 0)
    col = iota((2 * LANES, LANES), 1)
    upper = src // LANES
    src = src & (LANES - 1)
    src_t = src & (SUBS - 1)
    src_q = (src & (edge - 1)) // SUBS
    to_z = ((src_t & 3) * 2 + src // (2 * edge)) * half + upper * SUBS + (src_t // 4) * 4 + src_q
    to_y = upper * (LANES // 2) + src // 2
    pool_z = jnp.where(col == to_z, 0.125, 0.0).astype(jnp.bfloat16)
    pool_y = jnp.where(col == to_y, 0.125, 0.0).astype(jnp.bfloat16)

    for d in range(1, line):
        rep_copies[d].wait_recv()
    for b in range(boxes):
        for g in range(6):
            ghost_all = replies[ghost_at[b * 6 + g]]
            own_all = table[b * 6 + g]
            normal = g // 2 + 1
            pair = []
            for layers in (ghost_all, own_all):
                u = [layers[c * SUBS : (c + 1) * SUBS, :] for c in range(5)]
                pair.append((u,) + physical(u, primitives(u), normal))
            if g % 2:
                flux = twice_flux(pair[1], pair[0])
                scale = -0.5 * COURANT
            else:
                flux = twice_flux(pair[0], pair[1])
                scale = 0.5 * COURANT
            for c in range(5):
                flux_d[pl.ds(((b * 6 + g) * 5 + c) * SUBS, SUBS), :] = scale * flux[c]

    for b in range(boxes):
        at = b * 6 * 5 * SUBS
        parts = [flux_d[pl.ds(at + e, 20, stride=4), :] for e in range(4)]
        pooled[b, 0:20, :] = split_dot(jnp.concatenate(parts, axis=1), shrink, 2)
        for g, pool in ((2, pool_y), (4, pool_z)):
            parts = []
            for f in (g, g + 1):
                at = (b * 6 + f) * 5 * SUBS
                parts.append(flux_d[pl.ds(at, 20, stride=2), :] + flux_d[pl.ds(at + 1, 20, stride=2), :])
            pooled[b, 10 * g : 10 * g + 20, :] = split_dot(jnp.concatenate(parts, axis=1), pool, 2)
        pooled[b, 60:64, :] = jnp.zeros((4, LANES), f32)
    for d in range(columns):
        if d:
            pool_send[d] = pooled[sent_box[d]]
            rx_copies[d, 2] = pltpu.make_async_remote_copy(
                pool_send.at[d], pool_recv.at[d], rx_ss.at[d * 3 + 2], rx_rs.at[d * 3 + 2],
                device_id=col_dev(lax.rem(gx + columns - d, columns)), device_id_type=MESH,
            )
            rx_copies[d, 2].start()
        else:
            pool_recv[d] = pooled[sent_box[0]]

    def add_faces(bc, carry):
        b = lax.div(bc, 5)
        c = bc - b * 5
        row = pl.multiple_of(bc * edge, edge)
        d = [
            flux_d[pl.ds(pl.multiple_of(((b * 6 + g) * 5 + c) * SUBS, SUBS), SUBS), :]
            for g in range(6)
        ]
        for q in range(quarters):
            for t in range(tiles):
                s = q * SUBS + t
                at = (t, pl.ds(row + q * SUBS, SUBS), slice(None))
                block = nxt_state[at]
                block = block + jnp.where(
                    in_edge == 0,
                    pltpu.roll(d[4], (-s) % LANES, 1),
                    jnp.where(in_edge == edge - 1, pltpu.roll(d[5], (edge - 1 - s) % LANES, 1), 0.0),
                )
                if t == 0:
                    block = block + jnp.where(group == 0, pltpu.roll(d[2], (-q * edge) % LANES, 1), 0.0)
                if t == tiles - 1:
                    block = block + jnp.where(
                        group == per_tile - 1,
                        pltpu.roll(d[3], (LANES - edge - q * edge) % LANES, 1),
                        0.0,
                    )
                if q == 0:
                    block = block + jnp.where(sub8 == 0, d[0][t : t + 1, :], 0.0)
                if q == quarters - 1:
                    block = block + jnp.where(sub8 == SUBS - 1, d[1][t : t + 1, :], 0.0)
                nxt_state[at] = block
        return carry

    lax.fori_loop(0, boxes * 5, add_faces, 0)

    stores = []
    for t in range(tiles):
        stores.append(
            pltpu.make_async_copy(nxt_state.at[t], fine_out.at[:, tile_at(t)], out_sem.at[1 + t])
        )
        stores[-1].start()

    wide20 = iota((20, LANES), 1)
    low_z = (wide20 & (half - 1)) == 0
    high_z = (wide20 & (half - 1)) == half - 1
    low_y = wide20 < half
    high_y = wide20 >= LANES - half
    for d in range(columns):
        if d:
            for h in range(3):
                rx_copies[d, h].wait_recv()
        x, y, z = (pool_recv[d, pl.ds(20 * i, 20), :] for i in range(3))
        for h in range(2):
            adds = []
            for q in range(quarters):
                s = h * 4 + q
                add = jnp.where(
                    low_z,
                    pltpu.roll(z, (-s) % LANES, 1),
                    jnp.where(high_z, pltpu.roll(z, (half - 1 - SUBS - s) % LANES, 1), 0.0),
                )
                if h:
                    shift = (LANES - half - LANES // 2 - half * q) % LANES
                    add = add + jnp.where(high_y, pltpu.roll(y, shift, 1), 0.0)
                else:
                    add = add + jnp.where(low_y, pltpu.roll(y, (-half * q) % LANES, 1), 0.0)
                adds.append(add)
            for c in range(5):
                for f in range(2):
                    source = (f * 5 + c) * 2 + h
                    add = jnp.concatenate(
                        [part[4 * c : 4 * c + 4, :] for part in adds[2 * f : 2 * f + 2]], axis=0
                    )
                    add = add + jnp.where(sub8 == f * (SUBS - 1), x[source : source + 1, :], 0.0)
                    at = c * half + f * SUBS
                    rx_recv[d, h, at : at + SUBS, :] = rx_recv[d, h, at : at + SUBS, :] + add
    for c in range(blocks):
        part = pl.ds(c * 5 * half, 5 * half)
        taken = rx_recv[cover_at[c]]
        for h in range(2):
            coarse_next[part, tile_at(h)] = jnp.where(cover_flag[c] > 0, taken[h], coarse[h, part, :])
    store_coarse = pltpu.make_async_copy(coarse_next, coarse_out, out_sem.at[0])
    store_coarse.start()

    for copies in (req_copies, reqx_copies, rep_copies, rx_copies):
        for d in copies:
            copies[d].wait_send()
    for store in stores:
        store.wait()
    store_coarse.wait()


def body(fine_state, coarse_state, neighbours, coarse_sources, covering):
    boxes, comps, edge, plane = fine_state.shape
    blocks, _, half, small = coarse_state.shape
    line = lax.axis_size("gy") * lax.axis_size("gz")
    columns = lax.axis_size("gx")
    faces = boxes * 6
    slots = -(-faces // line)
    dims = (line, columns, lax.axis_size("gz"), boxes, blocks, edge, half, slots)
    fine_rows = boxes * comps * edge
    coarse_rows = blocks * comps * half
    f32, i32 = jnp.float32, jnp.int32
    vmem = pltpu.VMEM
    dma = pltpu.SemaphoreType.DMA
    layer = (comps * SUBS, LANES)
    fine_next, coarse_next = pl.pallas_call(
        functools.partial(kernel, dims),
        out_shape=(
            pltpu.VMEM((fine_rows, plane), f32),
            pltpu.VMEM((coarse_rows, small), f32),
        ),
        in_specs=[pl.BlockSpec(memory_space=pltpu.HBM)] * 5,
        out_specs=(pl.BlockSpec(memory_space=pl.ANY),) * 2,
        scratch_shapes=[
            vmem((plane // LANES, fine_rows, LANES), f32),
            vmem((2, coarse_rows, LANES), f32),
            vmem((plane // LANES, fine_rows, LANES), f32),
            vmem((faces + 6 * blocks,) + layer, f32),
            vmem((2, 2 * coarse_rows, LANES), f32),
            vmem((2, blocks * comps * SUBS, LANES), f32),
            vmem((faces * comps * SUBS, LANES), f32),
            vmem((boxes, 2, comps * half, LANES), f32),
            vmem((coarse_rows, small), f32),
            vmem((boxes, 6), i32),
            vmem((boxes, 6), i32),
            vmem((1, blocks), i32),
            vmem((24, LANES), i32),
            vmem((line, SUBS, LANES), i32),
            vmem((line, SUBS, LANES), i32),
            vmem((columns, SUBS, LANES), i32),
            vmem((columns, SUBS, LANES), i32),
            vmem((line, slots) + layer, f32),
            vmem((line * slots,) + layer, f32),
            vmem((columns, 2, comps * half, LANES), f32),
            vmem((columns, 2, comps * half, LANES), f32),
            vmem((boxes, comps, edge, LANES), f32),
            vmem((boxes, 64, LANES), f32),
            vmem((columns, 64, LANES), f32),
            vmem((columns, 64, LANES), f32),
            dma((5 + plane // LANES,)),
            dma((1 + plane // LANES,)),
        ]
        + [dma((line,)), dma((line,)), dma((columns,)), dma((columns,))]
        + [dma((line,)), dma((line,)), dma((3 * columns,)), dma((3 * columns,))],
        compiler_params=pltpu.CompilerParams(
            collective_id=0, has_side_effects=True, vmem_limit_bytes=60 * 1024 * 1024
        ),
    )(
        fine_state.reshape(fine_rows, plane),
        coarse_state.reshape(coarse_rows, small),
        neighbours,
        coarse_sources,
        covering.reshape(1, blocks),
    )
    return fine_next.reshape(fine_state.shape), coarse_next.reshape(coarse_state.shape)


def solution(mesh):
    spec = ("gx", "gy", "gz")
    wide = P(spec, None, None, None)
    return jax.shard_map(
        body,
        mesh=mesh,
        in_specs=(wide, wide, P(spec, None), P(spec, None), P(spec)),
        out_specs=(wide, wide),
        check_vma=False,
    )
```

```python
import functools
import jax
import jax.numpy as jnp
from jax import lax
from jax.experimental import pallas as pl
from jax.experimental.pallas import tpu as pltpu
from jax.sharding import PartitionSpec as P

GAMMA = 5.0 / 3.0
COURANT = 0.12
LANES = 128
SUBS = 8
MESH = pl.DeviceIdType.MESH


def primitives(u):
    inverse = 1.0 / u[0]
    speeds = [u[1] * inverse, u[2] * inverse, u[3] * inverse]
    kinetic = 0.5 * (u[1] * speeds[0] + u[2] * speeds[1] + u[3] * speeds[2])
    pressure = (GAMMA - 1.0) * (u[4] - kinetic)
    square = GAMMA * pressure * inverse
    return speeds, pressure, square * lax.rsqrt(square)


def physical(u, prim, normal):
    speeds, pressure, sound = prim
    across = speeds[normal - 1]
    f = [u[normal], u[1] * across, u[2] * across, u[3] * across, (u[4] + pressure) * across]
    f[normal] = f[normal] + pressure
    return f, jnp.abs(across) + sound


def twice_flux(left, right):
    (ul, fl, sl), (ur, fr, sr) = left, right
    fastest = jnp.maximum(sl, sr)
    return [(a + b) - fastest * (d - c) for a, b, c, d in zip(fl, fr, ul, ur)]


def moved(u, f, s, normal, move):
    ud = [move(x) for x in u]
    fd = [ud[normal] if k == 0 else move(f[k]) for k in range(5)]
    return ud, fd, move(s)


def split_dot(x, table, terms):
    total = None
    for term in range(terms):
        part = x.astype(jnp.bfloat16)
        if term < terms - 1:
            x = x - part.astype(jnp.float32)
        add = jnp.dot(part, table, preferred_element_type=jnp.float32)
        total = add if total is None else total + add
    return total


def iota(shape, dim):
    return lax.broadcasted_iota(jnp.int32, shape, dim)


def lane_total(x):
    for shift in (1, 2, 4, 8, 16, 32, 64):
        x = x + pltpu.roll(x, shift, 1)
    return x


def kernel(
    dims,
    fine_hbm, coarse_hbm, neigh_hbm, csrc_hbm, cov_hbm,
    fine_out, coarse_out,
    fine, coarse, nxt_state, table, widened, rows_y, flux_d, restr,
    neigh, csrc, cov, ids, req_send, req_recv, reqx_send, reqx_recv, rep_send, replies, rx_send, rx_recv,
    carried, pooled, pool_send, pool_recv,
    in_sem, out_sem, req_ss, req_rs, reqx_ss, reqx_rs, rep_ss, rep_rs, rx_ss, rx_rs,
):
    line, columns, gz_size, boxes, blocks, edge, half, slots = dims
    f32, i32 = jnp.float32, jnp.int32
    plane = edge * edge
    tiles = plane // LANES
    quarters = edge // SUBS
    faces = boxes * 6
    per_tile = LANES // edge
    gx = lax.axis_index("gx")
    gy = lax.axis_index("gy")
    gz = lax.axis_index("gz")
    me = gy * gz_size + gz

    def line_dev(p):
        return (gx, lax.div(p, gz_size), lax.rem(p, gz_size))

    def col_dev(x):
        return (x, gy, gz)

    def tile_at(t):
        return pl.ds(t * LANES, LANES)

    load_fine = [
        pltpu.make_async_copy(fine_hbm.at[:, tile_at(t)], fine.at[t], in_sem.at[5 + t])
        for t in range(tiles)
    ]
    load_coarse = [
        pltpu.make_async_copy(coarse_hbm.at[:, tile_at(t)], coarse.at[t], in_sem.at[t])
        for t in range(2)
    ]
    load_ids = [
        pltpu.make_async_copy(a, b, in_sem.at[2 + i])
        for i, (a, b) in enumerate(((neigh_hbm, neigh), (csrc_hbm, csrc), (cov_hbm, cov)))
    ]
    for load in load_ids:
        load.start()
    for load in load_fine + load_coarse:
        load.start()

    barrier = pltpu.get_barrier_semaphore()
    for d in range(1, line):
        pl.semaphore_signal(barrier, 1, device_id=line_dev(lax.rem(me + d, line)), device_id_type=MESH)
    for d in range(1, columns):
        pl.semaphore_signal(barrier, 1, device_id=col_dev(lax.rem(gx + d, columns)), device_id_type=MESH)

    for load in load_ids:
        load.wait()
    ids[...] = jnp.full((24, LANES), -1, i32)
    ids[0:boxes, 0:6] = neigh[...]
    ids[8 : 8 + boxes, 0:6] = csrc[...]
    ids[16:17, 0:blocks] = cov[...]
    lane8 = iota((SUBS, LANES), 1)
    sub8 = iota((SUBS, LANES), 0)

    def in_row(tile):
        row = tile[0:1, :]
        for b in range(1, boxes):
            lane1 = lane8[0:1, :]
            row = jnp.where(lane1 >= 6 * b, pltpu.roll(tile, 6 * b, 1)[b : b + 1, :], row)
        return jnp.broadcast_to(row, (line, LANES))

    lane = iota((line, LANES), 1)
    sub = iota((line, LANES), 0)
    near = in_row(ids[0:8, :])
    far = in_row(ids[8:16, :])
    is_fine = near >= 0
    near_dev = lax.div(near, jnp.full_like(near, boxes))
    far_dev = lax.div(far, jnp.full_like(far, blocks))
    side = lane
    for b in range(1, boxes):
        side = jnp.where(lane >= 6 * b, lane - 6 * b, side)
    facing = jnp.bitwise_xor(side, 1)
    code = jnp.where(
        is_fine,
        (near - near_dev * boxes) * 6 + facing,
        faces + (far - far_dev * blocks) * 6 + facing,
    )
    away = jnp.where(is_fine, near_dev, far_dev) - gx * line - me
    away = jnp.where(away < 0, away + line, away)
    match = (away == sub) & (lane < faces)
    ones = jnp.where(match, 1, 0)
    run = ones
    for shift in (1, 2, 4, 8):
        run = run + jnp.where(lane >= shift, pltpu.roll(run, shift, 1), 0)
    rank = run - ones
    asked = jnp.zeros((line, LANES), i32)
    for k in range(slots):
        asked = jnp.where(lane == k, lane_total(jnp.where(match & (rank == k), code, 0)), asked)
    for d in range(line):
        req_send[d] = jnp.broadcast_to(asked[d : d + 1, :], (SUBS, LANES))
    place = jnp.where(match & (rank < slots), sub * slots + rank, 0)
    place_tile = place[0:SUBS, :]
    for part in range(1, line // SUBS):
        place_tile = place_tile + place[part * SUBS : (part + 1) * SUBS, :]
    for shift in (1, 2, 4):
        place_tile = place_tile + pltpu.roll(place_tile, shift, 0)

    place_row = place_tile[0:1, :]
    ghost_at = [place_row[0, i] for i in range(faces)]
    own_codes = [asked[0:1, :][0, k] for k in range(slots)]

    cover = jnp.broadcast_to(ids[16:17, :], (SUBS, LANES))
    cover_dev = lax.div(cover, jnp.full_like(cover, boxes))
    cover_col = lax.div(cover_dev, jnp.full_like(cover, line)) - gx
    cover_col = jnp.where(cover_col < 0, cover_col + columns, cover_col)
    covered = cover >= 0
    wanted = lane_total(
        jnp.where(covered & (cover_col == sub8), cover - cover_dev * boxes, 0)
    )
    for d in range(columns):
        reqx_send[d] = jnp.broadcast_to(wanted[d : d + 1, :], (SUBS, LANES))
    cover_col = jnp.where(covered, cover_col, 0)
    covered = jnp.where(covered, 1, 0)
    cover_at = [cover_col[0:1, :][0, c] for c in range(blocks)]
    cover_flag = [covered[0:1, :][0, c] for c in range(blocks)]
    sent_box = [wanted[0:1, :][0, 0]]

    in_edge = lane8 & (edge - 1)
    group = lane8 // edge
    pl.semaphore_wait(barrier, line - 1 + columns - 1)

    req_copies = {}
    for d in range(1, line):
        req_copies[d] = pltpu.make_async_remote_copy(
            req_send.at[d], req_recv.at[d], req_ss.at[d], req_rs.at[d],
            device_id=line_dev(lax.rem(me + d, line)), device_id_type=MESH,
        )
        req_copies[d].start()
    reqx_copies = {}
    for d in range(1, columns):
        reqx_copies[d] = pltpu.make_async_remote_copy(
            reqx_send.at[d], reqx_recv.at[d], reqx_ss.at[d], reqx_rs.at[d],
            device_id=col_dev(lax.rem(gx + d, columns)), device_id_type=MESH,
        )
        reqx_copies[d].start()

    src = iota((4 * LANES, LANES), 0)
    col = iota((4 * LANES, LANES), 1)
    shrink = jnp.where(
        ((src // (2 * edge)) == col // half) & ((src & (edge - 1)) // 2 == (col & (half - 1))),
        0.125,
        0.0,
    ).astype(jnp.bfloat16)

    tall_lane = iota((edge, LANES), 1)
    tall_row = iota((edge, LANES), 0)
    not_last_x = tall_row < edge - 1
    not_last_z = (tall_lane & (edge - 1)) < edge - 1

    def box_step(half_box, b):
        def load(t):
            return [
                fine[t, pl.ds(pl.multiple_of((b * 5 + c) * edge, edge), edge), :]
                for c in range(5)
            ]

        first = half_box * (tiles // 2)
        cur = load(first)
        prim = primitives(cur)
        if half_box:
            before = [carried[b, c] for c in range(5)]
        else:
            before = [jnp.zeros((edge, LANES), f32)] * 5
        for t in range(first, first + tiles // 2):
            if t < tiles - 1:
                after = load(t + 1)
                after_prim = primitives(after)
            else:
                after, after_prim = cur, prim
            f, s = physical(cur, prim, 1)
            right = moved(cur, f, s, 1, lambda x: pltpu.roll(x, edge - 1, 0))
            flux = [jnp.where(not_last_x, x, 0.0) for x in twice_flux((cur, f, s), right)]
            step = [x - pltpu.roll(x, 1, 0) for x in flux]
            f, s = physical(cur, prim, 3)
            right = moved(cur, f, s, 3, lambda x: pltpu.roll(x, LANES - 1, 1))
            flux = [jnp.where(not_last_z, x, 0.0) for x in twice_flux((cur, f, s), right)]
            step = [a + (x - pltpu.roll(x, 1, 1)) for a, x in zip(step, flux)]
            f, s = physical(cur, prim, 2)
            fa, sa = physical(after, after_prim, 2)

            def up(here, there):
                return pltpu.roll(jnp.where(tall_lane < edge, there, here), LANES - edge, 1)

            ud = [up(x, y) for x, y in zip(cur, after)]
            fd = [ud[2]] + [up(x, y) for x, y in zip(f[1:], fa[1:])]
            flux = twice_flux((cur, f, s), (ud, fd, up(s, sa)))
            if t == tiles - 1:
                flux = [jnp.where(tall_lane < LANES - edge, x, 0.0) for x in flux]
            for c in range(5):
                low = pltpu.roll(
                    jnp.where(tall_lane >= LANES - edge, before[c], flux[c]), edge, 1
                )
                total = step[c] + (flux[c] - low)
                nxt_state[t, pl.ds(pl.multiple_of((b * 5 + c) * edge, edge), edge), :] = (
                    cur[c] - (0.5 * COURANT) * total
                )
            before = flux
            cur, prim = after, after_prim
        if not half_box:
            for c in range(5):
                carried[b, c] = before[c]

    pairs = 5 * half
    rx_copies = {}

    def step_half(h):
        def one_box(b, carry):
            box_step(h, b)
            start = b * 5 * edge
            parts = [
                nxt_state[t, pl.ds(start, pairs, stride=2), :]
                + nxt_state[t, pl.ds(start + 1, pairs, stride=2), :]
                for t in range(4 * h, 4 * h + 4)
            ]
            restr[b, h] = split_dot(jnp.concatenate(parts, axis=1), shrink, 2)
            return carry

        lax.fori_loop(0, boxes, one_box, 0)

    def send_half(h):
        for d in range(columns):
            if d:
                rx_send[d, h] = restr[sent_box[d], h]
                rx_copies[d, h] = pltpu.make_async_remote_copy(
                    rx_send.at[d, h], rx_recv.at[d, h], rx_ss.at[d * 3 + h], rx_rs.at[d * 3 + h],
                    device_id=col_dev(lax.rem(gx + columns - d, columns)), device_id_type=MESH,
                )
                rx_copies[d, h].start()
            else:
                rx_recv[d, h] = restr[sent_box[0], h]

    for load in load_fine:
        load.wait()
    step_half(0)

    for d in range(1, columns):
        reqx_copies[d].wait_recv()
    sent_box += [reqx_recv[d][0:1, :][0, 0] for d in range(1, columns)]
    send_half(0)


    def fine_layers(bc, carry):
        b = lax.div(bc, 5)
        c = bc - b * 5
        row = pl.multiple_of(bc * edge, edge)
        z_low = jnp.zeros((SUBS, LANES), f32)
        z_high = jnp.zeros((SUBS, LANES), f32)
        y_low = jnp.zeros((SUBS, LANES), f32)
        y_high = jnp.zeros((SUBS, LANES), f32)
        for q in range(quarters):
            for t in range(tiles):
                block = fine[t, pl.ds(row + q * SUBS, SUBS), :]
                s = q * SUBS + t
                z_low = jnp.where(in_edge == s, pltpu.roll(block, s, 1), z_low)
                z_high = jnp.where(in_edge == s, pltpu.roll(block, (s - edge + 1) % LANES, 1), z_high)
                if t == 0:
                    y_low = jnp.where(group == q, pltpu.roll(block, q * edge, 1), y_low)
                if t == tiles - 1:
                    y_high = jnp.where(
                        group == q, pltpu.roll(block, (q * edge - (LANES - edge)) % LANES, 1), y_high
                    )
        at = pl.ds(pl.multiple_of(c * SUBS, SUBS), SUBS)
        for side, layer in enumerate((y_low, y_high, z_low, z_high)):
            table[b * 6 + 2 + side, at, :] = layer
        return carry

    lax.fori_loop(0, boxes * 5, fine_layers, 0, unroll=2)
    for b in range(boxes):
        for f in range(2):
            for t in range(tiles):
                table[b * 6 + f, pl.ds(t, 5, stride=SUBS), :] = fine[
                    t, pl.ds(b * 5 * edge + f * (edge - 1), 5, stride=edge), :
                ]

    for load in load_coarse:
        load.wait()
    small = half * half
    src = iota((small, 2 * LANES), 0)
    col = iota((small, 2 * LANES), 1)
    lane_w = col & (LANES - 1)
    y_src = (lane_w // edge) * ((half - 1) * half) + (lane_w & (edge - 1)) // 2
    z_j = 4 * (lane_w & (SUBS - 1)) + lane_w // edge
    z_src = (z_j // 2) * half + ((lane_w & (edge - 1)) // SUBS) * (half - 1)
    y_ok = (col < LANES) & (lane_w < 2 * edge) & (src == y_src)
    z_ok = (col >= LANES) & ((lane_w & (edge - 1)) < 2 * SUBS) & (src == z_src)
    lateral_table = jnp.where(y_ok | z_ok, 1.0, 0.0).astype(jnp.bfloat16)
    lateral = split_dot(jnp.concatenate([coarse[0], coarse[1]], axis=1), lateral_table, 3)
    rows = blocks * 5 * half
    for part in range(2):
        piece = lateral[:, part * LANES : (part + 1) * LANES]
        widened[part, pl.ds(0, rows, stride=2), :] = piece
        widened[part, pl.ds(1, rows, stride=2), :] = piece
    z_group = in_edge // SUBS

    def coarse_layers(bc, carry):
        b = lax.div(bc, 5)
        c = bc - b * 5
        row = pl.multiple_of(bc * edge, edge)
        for f in range(2):
            y = jnp.zeros((SUBS, LANES), f32)
            z = jnp.zeros((SUBS, LANES), f32)
            for q in range(quarters):
                block = widened[0, pl.ds(row + q * SUBS, SUBS), :]
                y = jnp.where(group == q, pltpu.roll(block, (edge * (q - f)) % LANES, 1), y)
                block = widened[1, pl.ds(row + q * SUBS, SUBS), :]
                z = jnp.where(z_group == q, pltpu.roll(block, (SUBS * (q - f)) % LANES, 1), z)
            at = pl.ds(pl.multiple_of(c * SUBS, SUBS), SUBS)
            table[faces + b * 6 + 2 + f, at, :] = y
            table[faces + b * 6 + 4 + f, at, :] = z
        return carry

    lax.fori_loop(0, blocks * 5, coarse_layers, 0, unroll=4)

    src = iota((LANES, LANES), 0)
    col = iota((LANES, LANES), 1)
    x_table = jnp.where(
        src == (col // (2 * edge)) * half + (col & (edge - 1)) // 2, 1.0, 0.0
    ).astype(jnp.bfloat16)
    for f in range(2):
        for t in range(SUBS):
            ends = coarse[t // 4, pl.ds(f * (half - 1), blocks * 5, stride=half), :]
            rows_y[f, pl.ds(t, blocks * 5, stride=SUBS), :] = pltpu.roll(
                ends, (-2 * half * (t % 4)) % LANES, 1
            )
        spread = split_dot(rows_y[f], x_table, 3)
        for b in range(blocks):
            at = b * 5 * SUBS
            table[faces + b * 6 + f] = spread[at : at + 5 * SUBS, :]

    rep_copies = {}
    for d in range(1, line):
        req_copies[d].wait_recv()
    codes = [own_codes] + [
        [req_recv[d][0:1, :][0, k] for k in range(slots)] for d in range(1, line)
    ]
    for d in list(range(1, line)) + [0]:
        for k in range(slots):
            layer = table[codes[d][k]]
            if d:
                rep_send[d, k] = layer
            else:
                replies[d * slots + k] = layer
        if d:
            rep_copies[d] = pltpu.make_async_remote_copy(
                rep_send.at[d], replies.at[pl.ds(d * slots, slots)], rep_ss.at[d], rep_rs.at[d],
                device_id=line_dev(lax.rem(me + line - d, line)), device_id_type=MESH,
            )
            rep_copies[d].start()

    step_half(1)
    send_half(1)

    src = iota((2 * LANES, LANES), 0)
    col = iota((2 * LANES, LANES), 1)
    upper = src // LANES
    src = src & (LANES - 1)
    src_t = src & (SUBS - 1)
    src_q = (src & (edge - 1)) // SUBS
    to_z = ((src_t & 3) * 2 + src // (2 * edge)) * half + upper * SUBS + (src_t // 4) * 4 + src_q
    to_y = upper * (LANES // 2) + src // 2
    pool_z = jnp.where(col == to_z, 0.125, 0.0).astype(jnp.bfloat16)
    pool_y = jnp.where(col == to_y, 0.125, 0.0).astype(jnp.bfloat16)

    for d in range(1, line):
        rep_copies[d].wait_recv()
    for b in range(boxes):
        for g in range(6):
            ghost_all = replies[ghost_at[b * 6 + g]]
            own_all = table[b * 6 + g]
            normal = g // 2 + 1
            pair = []
            for layers in (ghost_all, own_all):
                u = [layers[c * SUBS : (c + 1) * SUBS, :] for c in range(5)]
                pair.append((u,) + physical(u, primitives(u), normal))
            if g % 2:
                flux = twice_flux(pair[1], pair[0])
                scale = -0.5 * COURANT
            else:
                flux = twice_flux(pair[0], pair[1])
                scale = 0.5 * COURANT
            for c in range(5):
                flux_d[pl.ds(((b * 6 + g) * 5 + c) * SUBS, SUBS), :] = scale * flux[c]

    for b in range(boxes):
        at = b * 6 * 5 * SUBS
        parts = [flux_d[pl.ds(at + e, 20, stride=4), :] for e in range(4)]
        pooled[b, 0:20, :] = split_dot(jnp.concatenate(parts, axis=1), shrink, 2)
        for g, pool in ((2, pool_y), (4, pool_z)):
            parts = []
            for f in (g, g + 1):
                at = (b * 6 + f) * 5 * SUBS
                parts.append(flux_d[pl.ds(at, 20, stride=2), :] + flux_d[pl.ds(at + 1, 20, stride=2), :])
            pooled[b, 10 * g : 10 * g + 20, :] = split_dot(jnp.concatenate(parts, axis=1), pool, 2)
        pooled[b, 60:64, :] = jnp.zeros((4, LANES), f32)
    for d in range(columns):
        if d:
            pool_send[d] = pooled[sent_box[d]]
            rx_copies[d, 2] = pltpu.make_async_remote_copy(
                pool_send.at[d], pool_recv.at[d], rx_ss.at[d * 3 + 2], rx_rs.at[d * 3 + 2],
                device_id=col_dev(lax.rem(gx + columns - d, columns)), device_id_type=MESH,
            )
            rx_copies[d, 2].start()
        else:
            pool_recv[d] = pooled[sent_box[0]]

    def add_faces(bc, carry):
        b = lax.div(bc, 5)
        c = bc - b * 5
        row = pl.multiple_of(bc * edge, edge)
        d = [
            flux_d[pl.ds(pl.multiple_of(((b * 6 + g) * 5 + c) * SUBS, SUBS), SUBS), :]
            for g in range(6)
        ]
        for q in range(quarters):
            for t in range(tiles):
                s = q * SUBS + t
                at = (t, pl.ds(row + q * SUBS, SUBS), slice(None))
                block = nxt_state[at]
                block = block + jnp.where(
                    in_edge == 0,
                    pltpu.roll(d[4], (-s) % LANES, 1),
                    jnp.where(in_edge == edge - 1, pltpu.roll(d[5], (edge - 1 - s) % LANES, 1), 0.0),
                )
                if t == 0:
                    block = block + jnp.where(group == 0, pltpu.roll(d[2], (-q * edge) % LANES, 1), 0.0)
                if t == tiles - 1:
                    block = block + jnp.where(
                        group == per_tile - 1,
                        pltpu.roll(d[3], (LANES - edge - q * edge) % LANES, 1),
                        0.0,
                    )
                if q == 0:
                    block = block + jnp.where(sub8 == 0, d[0][t : t + 1, :], 0.0)
                if q == quarters - 1:
                    block = block + jnp.where(sub8 == SUBS - 1, d[1][t : t + 1, :], 0.0)
                nxt_state[at] = block
        return carry

    lax.fori_loop(0, boxes * 5, add_faces, 0)

    stores = []
    for t in range(tiles):
        stores.append(
            pltpu.make_async_copy(nxt_state.at[t], fine_out.at[:, tile_at(t)], out_sem.at[1 + t])
        )
        stores[-1].start()

    wide20 = iota((20, LANES), 1)
    low_z = (wide20 & (half - 1)) == 0
    high_z = (wide20 & (half - 1)) == half - 1
    low_y = wide20 < half
    high_y = wide20 >= LANES - half
    for d in range(columns):
        if d:
            for h in range(3):
                rx_copies[d, h].wait_recv()
        x, y, z = (pool_recv[d, pl.ds(20 * i, 20), :] for i in range(3))
        for h in range(2):
            adds = []
            for q in range(quarters):
                s = h * 4 + q
                add = jnp.where(
                    low_z,
                    pltpu.roll(z, (-s) % LANES, 1),
                    jnp.where(high_z, pltpu.roll(z, (half - 1 - SUBS - s) % LANES, 1), 0.0),
                )
                if h:
                    shift = (LANES - half - LANES // 2 - half * q) % LANES
                    add = add + jnp.where(high_y, pltpu.roll(y, shift, 1), 0.0)
                else:
                    add = add + jnp.where(low_y, pltpu.roll(y, (-half * q) % LANES, 1), 0.0)
                adds.append(add)
            for c in range(5):
                for f in range(2):
                    source = (f * 5 + c) * 2 + h
                    add = jnp.concatenate(
                        [part[4 * c : 4 * c + 4, :] for part in adds[2 * f : 2 * f + 2]], axis=0
                    )
                    add = add + jnp.where(sub8 == f * (SUBS - 1), x[source : source + 1, :], 0.0)
                    at = c * half + f * SUBS
                    rx_recv[d, h, at : at + SUBS, :] = rx_recv[d, h, at : at + SUBS, :] + add
    for c in range(blocks):
        part = pl.ds(c * 5 * half, 5 * half)
        taken = rx_recv[cover_at[c]]
        for h in range(2):
            coarse_out[part, tile_at(h)] = jnp.where(cover_flag[c] > 0, taken[h], coarse[h, part, :])
    for copies in (req_copies, reqx_copies, rep_copies, rx_copies):
        for d in copies:
            copies[d].wait_send()
    for store in stores:
        store.wait()


def body(fine_state, coarse_state, neighbours, coarse_sources, covering):
    boxes, comps, edge, plane = fine_state.shape
    blocks, _, half, small = coarse_state.shape
    line = lax.axis_size("gy") * lax.axis_size("gz")
    columns = lax.axis_size("gx")
    faces = boxes * 6
    slots = -(-faces // line)
    dims = (line, columns, lax.axis_size("gz"), boxes, blocks, edge, half, slots)
    fine_rows = boxes * comps * edge
    coarse_rows = blocks * comps * half
    f32, i32 = jnp.float32, jnp.int32
    vmem = pltpu.VMEM
    dma = pltpu.SemaphoreType.DMA
    layer = (comps * SUBS, LANES)
    fine_next, coarse_next = pl.pallas_call(
        functools.partial(kernel, dims),
        out_shape=(
            pltpu.VMEM((fine_rows, plane), f32),
            pltpu.VMEM((coarse_rows, small), f32),
        ),
        in_specs=[pl.BlockSpec(memory_space=pltpu.HBM)] * 5,
        out_specs=(pl.BlockSpec(memory_space=pl.ANY), pl.BlockSpec(memory_space=pltpu.VMEM)),
        scratch_shapes=[
            vmem((plane // LANES, fine_rows, LANES), f32),
            vmem((2, coarse_rows, LANES), f32),
            vmem((plane // LANES, fine_rows, LANES), f32),
            vmem((faces + 6 * blocks,) + layer, f32),
            vmem((2, 2 * coarse_rows, LANES), f32),
            vmem((2, blocks * comps * SUBS, LANES), f32),
            vmem((faces * comps * SUBS, LANES), f32),
            vmem((boxes, 2, comps * half, LANES), f32),
            vmem((boxes, 6), i32),
            vmem((boxes, 6), i32),
            vmem((1, blocks), i32),
            vmem((24, LANES), i32),
            vmem((line, SUBS, LANES), i32),
            vmem((line, SUBS, LANES), i32),
            vmem((columns, SUBS, LANES), i32),
            vmem((columns, SUBS, LANES), i32),
            vmem((line, slots) + layer, f32),
            vmem((line * slots,) + layer, f32),
            vmem((columns, 2, comps * half, LANES), f32),
            vmem((columns, 2, comps * half, LANES), f32),
            vmem((boxes, comps, edge, LANES), f32),
            vmem((boxes, 64, LANES), f32),
            vmem((columns, 64, LANES), f32),
            vmem((columns, 64, LANES), f32),
            dma((5 + plane // LANES,)),
            dma((1 + plane // LANES,)),
        ]
        + [dma((line,)), dma((line,)), dma((columns,)), dma((columns,))]
        + [dma((line,)), dma((line,)), dma((3 * columns,)), dma((3 * columns,))],
        compiler_params=pltpu.CompilerParams(
            collective_id=0, has_side_effects=True, vmem_limit_bytes=60 * 1024 * 1024
        ),
    )(
        fine_state.reshape(fine_rows, plane),
        coarse_state.reshape(coarse_rows, small),
        neighbours,
        coarse_sources,
        covering.reshape(1, blocks),
    )
    return fine_next.reshape(fine_state.shape), coarse_next.reshape(coarse_state.shape)


def solution(mesh):
    spec = ("gx", "gy", "gz")
    wide = P(spec, None, None, None)
    return jax.shard_map(
        body,
        mesh=mesh,
        in_specs=(wide, wide, P(spec, None), P(spec, None), P(spec)),
        out_specs=(wide, wide),
        check_vma=False,
    )
```

```python
import functools
import jax
import jax.numpy as jnp
from jax import lax
from jax.experimental import pallas as pl
from jax.experimental.pallas import tpu as pltpu
from jax.sharding import PartitionSpec as P

GAMMA = 5.0 / 3.0
COURANT = 0.12
LANES = 128
SUBS = 8
MESH = pl.DeviceIdType.MESH


def primitives(u):
    inverse = 1.0 / u[0]
    speeds = [u[1] * inverse, u[2] * inverse, u[3] * inverse]
    kinetic = 0.5 * (u[1] * speeds[0] + u[2] * speeds[1] + u[3] * speeds[2])
    pressure = (GAMMA - 1.0) * (u[4] - kinetic)
    square = GAMMA * pressure * inverse
    return speeds, pressure, square * lax.rsqrt(square)


def physical(u, prim, normal):
    speeds, pressure, sound = prim
    across = speeds[normal - 1]
    f = [u[normal], u[1] * across, u[2] * across, u[3] * across, (u[4] + pressure) * across]
    f[normal] = f[normal] + pressure
    return f, jnp.abs(across) + sound


def twice_flux(left, right):
    (ul, fl, sl), (ur, fr, sr) = left, right
    fastest = jnp.maximum(sl, sr)
    return [(a + b) - fastest * (d - c) for a, b, c, d in zip(fl, fr, ul, ur)]


def moved(u, f, s, normal, move):
    ud = [move(x) for x in u]
    fd = [ud[normal] if k == 0 else move(f[k]) for k in range(5)]
    return ud, fd, move(s)


def split_dot(x, table, terms):
    total = None
    for term in range(terms):
        part = x.astype(jnp.bfloat16)
        if term < terms - 1:
            x = x - part.astype(jnp.float32)
        add = jnp.dot(part, table, preferred_element_type=jnp.float32)
        total = add if total is None else total + add
    return total


def iota(shape, dim):
    return lax.broadcasted_iota(jnp.int32, shape, dim)


def lane_total(x):
    for shift in (1, 2, 4, 8, 16, 32, 64):
        x = x + pltpu.roll(x, shift, 1)
    return x


def kernel(
    dims,
    fine_hbm, coarse_hbm, neigh_hbm, csrc_hbm, cov_hbm,
    fine_out, coarse_out,
    fine, coarse, nxt_state, table, widened, rows_y, flux_d, restr,
    neigh, csrc, cov, ids, req_send, req_recv, reqx_send, reqx_recv, rep_send, replies, rx_send, rx_recv,
    carried, pooled, pool_send, pool_recv,
    in_sem, out_sem, req_ss, req_rs, reqx_ss, reqx_rs, rep_ss, rep_rs, rx_ss, rx_rs,
):
    line, columns, gz_size, boxes, blocks, edge, half, slots = dims
    f32, i32 = jnp.float32, jnp.int32
    plane = edge * edge
    tiles = plane // LANES
    quarters = edge // SUBS
    faces = boxes * 6
    per_tile = LANES // edge
    gx = lax.axis_index("gx")
    gy = lax.axis_index("gy")
    gz = lax.axis_index("gz")
    me = gy * gz_size + gz

    def line_dev(p):
        return (gx, lax.div(p, gz_size), lax.rem(p, gz_size))

    def col_dev(x):
        return (x, gy, gz)

    def tile_at(t):
        return pl.ds(t * LANES, LANES)

    load_fine = [
        pltpu.make_async_copy(fine_hbm.at[:, tile_at(t)], fine.at[t], in_sem.at[5 + t])
        for t in range(tiles)
    ]
    load_coarse = [
        pltpu.make_async_copy(coarse_hbm.at[:, tile_at(t)], coarse.at[t], in_sem.at[t])
        for t in range(2)
    ]
    load_ids = [
        pltpu.make_async_copy(a, b, in_sem.at[2 + i])
        for i, (a, b) in enumerate(((neigh_hbm, neigh), (csrc_hbm, csrc), (cov_hbm, cov)))
    ]
    for load in load_ids:
        load.start()
    for load in load_fine + load_coarse:
        load.start()

    barrier = pltpu.get_barrier_semaphore()
    for d in range(1, line):
        pl.semaphore_signal(barrier, 1, device_id=line_dev(lax.rem(me + d, line)), device_id_type=MESH)
    for d in range(1, columns):
        pl.semaphore_signal(barrier, 1, device_id=col_dev(lax.rem(gx + d, columns)), device_id_type=MESH)

    for load in load_ids:
        load.wait()
    ids[...] = jnp.full((24, LANES), -1, i32)
    ids[0:boxes, 0:6] = neigh[...]
    ids[8 : 8 + boxes, 0:6] = csrc[...]
    ids[16:17, 0:blocks] = cov[...]
    lane8 = iota((SUBS, LANES), 1)
    sub8 = iota((SUBS, LANES), 0)

    def in_row(tile):
        row = tile[0:1, :]
        for b in range(1, boxes):
            lane1 = lane8[0:1, :]
            row = jnp.where(lane1 >= 6 * b, pltpu.roll(tile, 6 * b, 1)[b : b + 1, :], row)
        return jnp.broadcast_to(row, (line, LANES))

    lane = iota((line, LANES), 1)
    sub = iota((line, LANES), 0)
    near = in_row(ids[0:8, :])
    far = in_row(ids[8:16, :])
    is_fine = near >= 0
    near_dev = lax.div(near, jnp.full_like(near, boxes))
    far_dev = lax.div(far, jnp.full_like(far, blocks))
    side = lane
    for b in range(1, boxes):
        side = jnp.where(lane >= 6 * b, lane - 6 * b, side)
    facing = jnp.bitwise_xor(side, 1)
    code = jnp.where(
        is_fine,
        (near - near_dev * boxes) * 6 + facing,
        faces + (far - far_dev * blocks) * 6 + facing,
    )
    away = jnp.where(is_fine, near_dev, far_dev) - gx * line - me
    away = jnp.where(away < 0, away + line, away)
    match = (away == sub) & (lane < faces)
    ones = jnp.where(match, 1, 0)
    run = ones
    for shift in (1, 2, 4, 8):
        run = run + jnp.where(lane >= shift, pltpu.roll(run, shift, 1), 0)
    rank = run - ones
    asked = jnp.zeros((line, LANES), i32)
    for k in range(slots):
        asked = jnp.where(lane == k, lane_total(jnp.where(match & (rank == k), code, 0)), asked)
    for d in range(line):
        req_send[d] = jnp.broadcast_to(asked[d : d + 1, :], (SUBS, LANES))
    place = jnp.where(match & (rank < slots), sub * slots + rank, 0)
    place_tile = place[0:SUBS, :]
    for part in range(1, line // SUBS):
        place_tile = place_tile + place[part * SUBS : (part + 1) * SUBS, :]
    for shift in (1, 2, 4):
        place_tile = place_tile + pltpu.roll(place_tile, shift, 0)

    place_row = place_tile[0:1, :]
    ghost_at = [place_row[0, i] for i in range(faces)]
    own_codes = [asked[0:1, :][0, k] for k in range(slots)]

    cover = jnp.broadcast_to(ids[16:17, :], (SUBS, LANES))
    cover_dev = lax.div(cover, jnp.full_like(cover, boxes))
    cover_col = lax.div(cover_dev, jnp.full_like(cover, line)) - gx
    cover_col = jnp.where(cover_col < 0, cover_col + columns, cover_col)
    covered = cover >= 0
    wanted = lane_total(
        jnp.where(covered & (cover_col == sub8), cover - cover_dev * boxes, 0)
    )
    for d in range(columns):
        reqx_send[d] = jnp.broadcast_to(wanted[d : d + 1, :], (SUBS, LANES))
    cover_col = jnp.where(covered, cover_col, 0)
    covered = jnp.where(covered, 1, 0)
    cover_at = [cover_col[0:1, :][0, c] for c in range(blocks)]
    cover_flag = [covered[0:1, :][0, c] for c in range(blocks)]
    sent_box = [wanted[0:1, :][0, 0]]

    in_edge = lane8 & (edge - 1)
    group = lane8 // edge
    pl.semaphore_wait(barrier, line - 1 + columns - 1)

    req_copies = {}
    for d in range(1, line):
        req_copies[d] = pltpu.make_async_remote_copy(
            req_send.at[d], req_recv.at[d], req_ss.at[d], req_rs.at[d],
            device_id=line_dev(lax.rem(me + d, line)), device_id_type=MESH,
        )
        req_copies[d].start()
    reqx_copies = {}
    for d in range(1, columns):
        reqx_copies[d] = pltpu.make_async_remote_copy(
            reqx_send.at[d], reqx_recv.at[d], reqx_ss.at[d], reqx_rs.at[d],
            device_id=col_dev(lax.rem(gx + d, columns)), device_id_type=MESH,
        )
        reqx_copies[d].start()

    src = iota((4 * LANES, LANES), 0)
    col = iota((4 * LANES, LANES), 1)
    shrink = jnp.where(
        ((src // (2 * edge)) == col // half) & ((src & (edge - 1)) // 2 == (col & (half - 1))),
        0.125,
        0.0,
    ).astype(jnp.bfloat16)

    tall_lane = iota((edge, LANES), 1)
    tall_row = iota((edge, LANES), 0)
    not_last_x = tall_row < edge - 1
    not_last_z = (tall_lane & (edge - 1)) < edge - 1

    def box_step(half_box, b):
        def load(t):
            return [
                fine[t, pl.ds(pl.multiple_of((b * 5 + c) * edge, edge), edge), :]
                for c in range(5)
            ]

        first = half_box * (tiles // 2)
        cur = load(first)
        prim = primitives(cur)
        if half_box:
            before = [carried[b, c] for c in range(5)]
        else:
            before = [jnp.zeros((edge, LANES), f32)] * 5
        for t in range(first, first + tiles // 2):
            if t < tiles - 1:
                after = load(t + 1)
                after_prim = primitives(after)
            else:
                after, after_prim = cur, prim
            f, s = physical(cur, prim, 1)
            right = moved(cur, f, s, 1, lambda x: pltpu.roll(x, edge - 1, 0))
            flux = [jnp.where(not_last_x, x, 0.0) for x in twice_flux((cur, f, s), right)]
            step = [x - pltpu.roll(x, 1, 0) for x in flux]
            f, s = physical(cur, prim, 3)
            right = moved(cur, f, s, 3, lambda x: pltpu.roll(x, LANES - 1, 1))
            flux = [jnp.where(not_last_z, x, 0.0) for x in twice_flux((cur, f, s), right)]
            step = [a + (x - pltpu.roll(x, 1, 1)) for a, x in zip(step, flux)]
            f, s = physical(cur, prim, 2)
            fa, sa = physical(after, after_prim, 2)

            def up(here, there):
                return pltpu.roll(jnp.where(tall_lane < edge, there, here), LANES - edge, 1)

            ud = [up(x, y) for x, y in zip(cur, after)]
            fd = [ud[2]] + [up(x, y) for x, y in zip(f[1:], fa[1:])]
            flux = twice_flux((cur, f, s), (ud, fd, up(s, sa)))
            if t == tiles - 1:
                flux = [jnp.where(tall_lane < LANES - edge, x, 0.0) for x in flux]
            for c in range(5):
                low = pltpu.roll(
                    jnp.where(tall_lane >= LANES - edge, before[c], flux[c]), edge, 1
                )
                total = step[c] + (flux[c] - low)
                nxt_state[t, pl.ds(pl.multiple_of((b * 5 + c) * edge, edge), edge), :] = (
                    cur[c] - (0.5 * COURANT) * total
                )
            before = flux
            cur, prim = after, after_prim
        if not half_box:
            for c in range(5):
                carried[b, c] = before[c]

    pairs = 5 * half
    rx_copies = {}

    def step_half(h):
        def one_box(b, carry):
            box_step(h, b)
            start = b * 5 * edge
            parts = [
                nxt_state[t, pl.ds(start, pairs, stride=2), :]
                + nxt_state[t, pl.ds(start + 1, pairs, stride=2), :]
                for t in range(4 * h, 4 * h + 4)
            ]
            restr[b, h] = split_dot(jnp.concatenate(parts, axis=1), shrink, 2)
            return carry

        lax.fori_loop(0, boxes, one_box, 0)

    def send_half(h):
        for d in range(columns):
            if d:
                rx_send[d, h] = restr[sent_box[d], h]
                rx_copies[d, h] = pltpu.make_async_remote_copy(
                    rx_send.at[d, h], rx_recv.at[d, h], rx_ss.at[d * 3 + h], rx_rs.at[d * 3 + h],
                    device_id=col_dev(lax.rem(gx + columns - d, columns)), device_id_type=MESH,
                )
                rx_copies[d, h].start()
            else:
                rx_recv[d, h] = restr[sent_box[0], h]

    for load in load_fine:
        load.wait()
    step_half(0)

    for d in range(1, columns):
        reqx_copies[d].wait_recv()
    sent_box += [reqx_recv[d][0:1, :][0, 0] for d in range(1, columns)]
    send_half(0)


    def fine_layers(bc, carry):
        b = lax.div(bc, 5)
        c = bc - b * 5
        row = pl.multiple_of(bc * edge, edge)
        z_low = jnp.zeros((SUBS, LANES), f32)
        z_high = jnp.zeros((SUBS, LANES), f32)
        y_low = jnp.zeros((SUBS, LANES), f32)
        y_high = jnp.zeros((SUBS, LANES), f32)
        for q in range(quarters):
            for t in range(tiles):
                block = fine[t, pl.ds(row + q * SUBS, SUBS), :]
                s = q * SUBS + t
                z_low = jnp.where(in_edge == s, pltpu.roll(block, s, 1), z_low)
                z_high = jnp.where(in_edge == s, pltpu.roll(block, (s - edge + 1) % LANES, 1), z_high)
                if t == 0:
                    y_low = jnp.where(group == q, pltpu.roll(block, q * edge, 1), y_low)
                if t == tiles - 1:
                    y_high = jnp.where(
                        group == q, pltpu.roll(block, (q * edge - (LANES - edge)) % LANES, 1), y_high
                    )
        at = pl.ds(pl.multiple_of(c * SUBS, SUBS), SUBS)
        for side, layer in enumerate((y_low, y_high, z_low, z_high)):
            table[b * 6 + 2 + side, at, :] = layer
        return carry

    lax.fori_loop(0, boxes * 5, fine_layers, 0, unroll=2)
    for b in range(boxes):
        for f in range(2):
            for t in range(tiles):
                table[b * 6 + f, pl.ds(t, 5, stride=SUBS), :] = fine[
                    t, pl.ds(b * 5 * edge + f * (edge - 1), 5, stride=edge), :
                ]

    for load in load_coarse:
        load.wait()
    small = half * half
    src = iota((small, 2 * LANES), 0)
    col = iota((small, 2 * LANES), 1)
    lane_w = col & (LANES - 1)
    y_src = (lane_w // edge) * ((half - 1) * half) + (lane_w & (edge - 1)) // 2
    z_j = 4 * (lane_w & (SUBS - 1)) + lane_w // edge
    z_src = (z_j // 2) * half + ((lane_w & (edge - 1)) // SUBS) * (half - 1)
    y_ok = (col < LANES) & (lane_w < 2 * edge) & (src == y_src)
    z_ok = (col >= LANES) & ((lane_w & (edge - 1)) < 2 * SUBS) & (src == z_src)
    lateral_table = jnp.where(y_ok | z_ok, 1.0, 0.0).astype(jnp.bfloat16)
    lateral = split_dot(jnp.concatenate([coarse[0], coarse[1]], axis=1), lateral_table, 2)
    rows = blocks * 5 * half
    for part in range(2):
        piece = lateral[:, part * LANES : (part + 1) * LANES]
        widened[part, pl.ds(0, rows, stride=2), :] = piece
        widened[part, pl.ds(1, rows, stride=2), :] = piece
    z_group = in_edge // SUBS

    def coarse_layers(bc, carry):
        b = lax.div(bc, 5)
        c = bc - b * 5
        row = pl.multiple_of(bc * edge, edge)
        for f in range(2):
            y = jnp.zeros((SUBS, LANES), f32)
            z = jnp.zeros((SUBS, LANES), f32)
            for q in range(quarters):
                block = widened[0, pl.ds(row + q * SUBS, SUBS), :]
                y = jnp.where(group == q, pltpu.roll(block, (edge * (q - f)) % LANES, 1), y)
                block = widened[1, pl.ds(row + q * SUBS, SUBS), :]
                z = jnp.where(z_group == q, pltpu.roll(block, (SUBS * (q - f)) % LANES, 1), z)
            at = pl.ds(pl.multiple_of(c * SUBS, SUBS), SUBS)
            table[faces + b * 6 + 2 + f, at, :] = y
            table[faces + b * 6 + 4 + f, at, :] = z
        return carry

    lax.fori_loop(0, blocks * 5, coarse_layers, 0, unroll=4)

    src = iota((LANES, LANES), 0)
    col = iota((LANES, LANES), 1)
    x_table = jnp.where(
        src == (col // (2 * edge)) * half + (col & (edge - 1)) // 2, 1.0, 0.0
    ).astype(jnp.bfloat16)
    for f in range(2):
        for t in range(SUBS):
            ends = coarse[t // 4, pl.ds(f * (half - 1), blocks * 5, stride=half), :]
            rows_y[f, pl.ds(t, blocks * 5, stride=SUBS), :] = pltpu.roll(
                ends, (-2 * half * (t % 4)) % LANES, 1
            )
        spread = split_dot(rows_y[f], x_table, 2)
        for b in range(blocks):
            at = b * 5 * SUBS
            table[faces + b * 6 + f] = spread[at : at + 5 * SUBS, :]

    rep_copies = {}
    for d in range(1, line):
        req_copies[d].wait_recv()
    codes = [own_codes] + [
        [req_recv[d][0:1, :][0, k] for k in range(slots)] for d in range(1, line)
    ]
    for d in list(range(1, line)) + [0]:
        for k in range(slots):
            layer = table[codes[d][k]]
            if d:
                rep_send[d, k] = layer
            else:
                replies[d * slots + k] = layer
        if d:
            rep_copies[d] = pltpu.make_async_remote_copy(
                rep_send.at[d], replies.at[pl.ds(d * slots, slots)], rep_ss.at[d], rep_rs.at[d],
                device_id=line_dev(lax.rem(me + line - d, line)), device_id_type=MESH,
            )
            rep_copies[d].start()

    step_half(1)
    send_half(1)

    src = iota((2 * LANES, LANES), 0)
    col = iota((2 * LANES, LANES), 1)
    upper = src // LANES
    src = src & (LANES - 1)
    src_t = src & (SUBS - 1)
    src_q = (src & (edge - 1)) // SUBS
    to_z = ((src_t & 3) * 2 + src // (2 * edge)) * half + upper * SUBS + (src_t // 4) * 4 + src_q
    to_y = upper * (LANES // 2) + src // 2
    pool_z = jnp.where(col == to_z, 0.125, 0.0).astype(jnp.bfloat16)
    pool_y = jnp.where(col == to_y, 0.125, 0.0).astype(jnp.bfloat16)

    for d in range(1, line):
        rep_copies[d].wait_recv()
    for b in range(boxes):
        for g in range(6):
            ghost_all = replies[ghost_at[b * 6 + g]]
            own_all = table[b * 6 + g]
            normal = g // 2 + 1
            pair = []
            for layers in (ghost_all, own_all):
                u = [layers[c * SUBS : (c + 1) * SUBS, :] for c in range(5)]
                pair.append((u,) + physical(u, primitives(u), normal))
            if g % 2:
                flux = twice_flux(pair[1], pair[0])
                scale = -0.5 * COURANT
            else:
                flux = twice_flux(pair[0], pair[1])
                scale = 0.5 * COURANT
            for c in range(5):
                flux_d[pl.ds(((b * 6 + g) * 5 + c) * SUBS, SUBS), :] = scale * flux[c]

    for b in range(boxes):
        at = b * 6 * 5 * SUBS
        parts = [flux_d[pl.ds(at + e, 20, stride=4), :] for e in range(4)]
        pooled[b, 0:20, :] = split_dot(jnp.concatenate(parts, axis=1), shrink, 2)
        for g, pool in ((2, pool_y), (4, pool_z)):
            parts = []
            for f in (g, g + 1):
                at = (b * 6 + f) * 5 * SUBS
                parts.append(flux_d[pl.ds(at, 20, stride=2), :] + flux_d[pl.ds(at + 1, 20, stride=2), :])
            pooled[b, 10 * g : 10 * g + 20, :] = split_dot(jnp.concatenate(parts, axis=1), pool, 2)
        pooled[b, 60:64, :] = jnp.zeros((4, LANES), f32)
    for d in range(columns):
        if d:
            pool_send[d] = pooled[sent_box[d]]
            rx_copies[d, 2] = pltpu.make_async_remote_copy(
                pool_send.at[d], pool_recv.at[d], rx_ss.at[d * 3 + 2], rx_rs.at[d * 3 + 2],
                device_id=col_dev(lax.rem(gx + columns - d, columns)), device_id_type=MESH,
            )
            rx_copies[d, 2].start()
        else:
            pool_recv[d] = pooled[sent_box[0]]

    def add_faces(bc, carry):
        b = lax.div(bc, 5)
        c = bc - b * 5
        row = pl.multiple_of(bc * edge, edge)
        d = [
            flux_d[pl.ds(pl.multiple_of(((b * 6 + g) * 5 + c) * SUBS, SUBS), SUBS), :]
            for g in range(6)
        ]
        for q in range(quarters):
            for t in range(tiles):
                s = q * SUBS + t
                at = (t, pl.ds(row + q * SUBS, SUBS), slice(None))
                block = nxt_state[at]
                block = block + jnp.where(
                    in_edge == 0,
                    pltpu.roll(d[4], (-s) % LANES, 1),
                    jnp.where(in_edge == edge - 1, pltpu.roll(d[5], (edge - 1 - s) % LANES, 1), 0.0),
                )
                if t == 0:
                    block = block + jnp.where(group == 0, pltpu.roll(d[2], (-q * edge) % LANES, 1), 0.0)
                if t == tiles - 1:
                    block = block + jnp.where(
                        group == per_tile - 1,
                        pltpu.roll(d[3], (LANES - edge - q * edge) % LANES, 1),
                        0.0,
                    )
                if q == 0:
                    block = block + jnp.where(sub8 == 0, d[0][t : t + 1, :], 0.0)
                if q == quarters - 1:
                    block = block + jnp.where(sub8 == SUBS - 1, d[1][t : t + 1, :], 0.0)
                nxt_state[at] = block
        return carry

    lax.fori_loop(0, boxes * 5, add_faces, 0)

    stores = []
    for t in range(tiles):
        stores.append(
            pltpu.make_async_copy(nxt_state.at[t], fine_out.at[:, tile_at(t)], out_sem.at[1 + t])
        )
        stores[-1].start()

    wide20 = iota((20, LANES), 1)
    low_z = (wide20 & (half - 1)) == 0
    high_z = (wide20 & (half - 1)) == half - 1
    low_y = wide20 < half
    high_y = wide20 >= LANES - half
    for d in range(columns):
        if d:
            for h in range(3):
                rx_copies[d, h].wait_recv()
        x, y, z = (pool_recv[d, pl.ds(20 * i, 20), :] for i in range(3))
        for h in range(2):
            adds = []
            for q in range(quarters):
                s = h * 4 + q
                add = jnp.where(
                    low_z,
                    pltpu.roll(z, (-s) % LANES, 1),
                    jnp.where(high_z, pltpu.roll(z, (half - 1 - SUBS - s) % LANES, 1), 0.0),
                )
                if h:
                    shift = (LANES - half - LANES // 2 - half * q) % LANES
                    add = add + jnp.where(high_y, pltpu.roll(y, shift, 1), 0.0)
                else:
                    add = add + jnp.where(low_y, pltpu.roll(y, (-half * q) % LANES, 1), 0.0)
                adds.append(add)
            for c in range(5):
                for f in range(2):
                    source = (f * 5 + c) * 2 + h
                    add = jnp.concatenate(
                        [part[4 * c : 4 * c + 4, :] for part in adds[2 * f : 2 * f + 2]], axis=0
                    )
                    add = add + jnp.where(sub8 == f * (SUBS - 1), x[source : source + 1, :], 0.0)
                    at = c * half + f * SUBS
                    rx_recv[d, h, at : at + SUBS, :] = rx_recv[d, h, at : at + SUBS, :] + add
    for c in range(blocks):
        part = pl.ds(c * 5 * half, 5 * half)
        taken = rx_recv[cover_at[c]]
        for h in range(2):
            coarse_out[part, tile_at(h)] = jnp.where(cover_flag[c] > 0, taken[h], coarse[h, part, :])
    for copies in (req_copies, reqx_copies, rep_copies, rx_copies):
        for d in copies:
            copies[d].wait_send()
    for store in stores:
        store.wait()


def body(fine_state, coarse_state, neighbours, coarse_sources, covering):
    boxes, comps, edge, plane = fine_state.shape
    blocks, _, half, small = coarse_state.shape
    line = lax.axis_size("gy") * lax.axis_size("gz")
    columns = lax.axis_size("gx")
    faces = boxes * 6
    slots = -(-faces // line)
    dims = (line, columns, lax.axis_size("gz"), boxes, blocks, edge, half, slots)
    fine_rows = boxes * comps * edge
    coarse_rows = blocks * comps * half
    f32, i32 = jnp.float32, jnp.int32
    vmem = pltpu.VMEM
    dma = pltpu.SemaphoreType.DMA
    layer = (comps * SUBS, LANES)
    fine_next, coarse_next = pl.pallas_call(
        functools.partial(kernel, dims),
        out_shape=(
            pltpu.VMEM((fine_rows, plane), f32),
            pltpu.VMEM((coarse_rows, small), f32),
        ),
        in_specs=[pl.BlockSpec(memory_space=pltpu.HBM)] * 5,
        out_specs=(pl.BlockSpec(memory_space=pl.ANY), pl.BlockSpec(memory_space=pltpu.VMEM)),
        scratch_shapes=[
            vmem((plane // LANES, fine_rows, LANES), f32),
            vmem((2, coarse_rows, LANES), f32),
            vmem((plane // LANES, fine_rows, LANES), f32),
            vmem((faces + 6 * blocks,) + layer, f32),
            vmem((2, 2 * coarse_rows, LANES), f32),
            vmem((2, blocks * comps * SUBS, LANES), f32),
            vmem((faces * comps * SUBS, LANES), f32),
            vmem((boxes, 2, comps * half, LANES), f32),
            vmem((boxes, 6), i32),
            vmem((boxes, 6), i32),
            vmem((1, blocks), i32),
            vmem((24, LANES), i32),
            vmem((line, SUBS, LANES), i32),
            vmem((line, SUBS, LANES), i32),
            vmem((columns, SUBS, LANES), i32),
            vmem((columns, SUBS, LANES), i32),
            vmem((line, slots) + layer, f32),
            vmem((line * slots,) + layer, f32),
            vmem((columns, 2, comps * half, LANES), f32),
            vmem((columns, 2, comps * half, LANES), f32),
            vmem((boxes, comps, edge, LANES), f32),
            vmem((boxes, 64, LANES), f32),
            vmem((columns, 64, LANES), f32),
            vmem((columns, 64, LANES), f32),
            dma((5 + plane // LANES,)),
            dma((1 + plane // LANES,)),
        ]
        + [dma((line,)), dma((line,)), dma((columns,)), dma((columns,))]
        + [dma((line,)), dma((line,)), dma((3 * columns,)), dma((3 * columns,))],
        compiler_params=pltpu.CompilerParams(
            collective_id=0, has_side_effects=True, vmem_limit_bytes=60 * 1024 * 1024
        ),
    )(
        fine_state.reshape(fine_rows, plane),
        coarse_state.reshape(coarse_rows, small),
        neighbours,
        coarse_sources,
        covering.reshape(1, blocks),
    )
    return fine_next.reshape(fine_state.shape), coarse_next.reshape(coarse_state.shape)


def solution(mesh):
    spec = ("gx", "gy", "gz")
    wide = P(spec, None, None, None)
    return jax.shard_map(
        body,
        mesh=mesh,
        in_specs=(wide, wide, P(spec, None), P(spec, None), P(spec)),
        out_specs=(wide, wide),
        check_vma=False,
    )
```
